32 devices in a mesh: groups: 2 (over y), expert: 8 (over z, core), blk: 2 (over x).
Axes of the slice: x: 2, y: 2, z: 4, core: 2. Of those that a mesh axis runs over, the one named last changes fastest.
Arguments:
- tokens: bfloat16 [128, 6144], P(('groups', 'expert'), 'blk'), parts along dimension 0, may hold values from -6 to 6
- expert_ids: int32 [128, 4], P(('groups', 'expert')), parts along dimension 0, may hold values from 0 to 7, all different within a row; in each aligned block of 8 rows (0 to 7, 8 to 15, ...) at most 5 rows name the same one
- route_weight: float32 [128, 4], P(('groups', 'expert')), parts along dimension 0, may hold values from 0.05 to 0.6
- w_gate: bfloat16 [8, 5376, 6144], P('expert', 'blk'), may hold values from -0.078125 to 0.078125
- w_up: bfloat16 [8, 5376, 6144], P('expert', 'blk'), may hold values from -0.078125 to 0.078125
- w_down: bfloat16 [8, 5376, 6144], P('expert', 'blk'), may hold values from -0.078125 to 0.078125
Outputs:
- mixed: bfloat16 [128, 6144], P(('groups', 'expert'), 'blk'), parts along dimension 0
The draws below stay inside these ranges and needn't reach their ends.
There are 2 independent parts, one for each index of `groups`. The reference program is written for one: setup_inputs(seed, part) draws one part's arguments, and reference() takes and returns one part's arrays. A program takes and returns all parts, laid end to end along the dimension named above; an argument that names none is the same for every part. Nothing has to cross between parts.
Inputs may be any that keep to these rules, and one draw needn't show every extreme that they name: `expert_ids`: each token names 4 different experts. In each aligned block of 8 rows (the tokens of one index of expert) no expert is named by more than 5 tokens, and in every draw some expert is named by exactly 5 tokens of some block.
All inputs are finite; a program needn't handle non-finite values.
Results may differ from the reference program's by a relative error of at most 0.0085.
Values may be sent and summed in bfloat16 or wider, within the bound.
No kernel may reach another device: no remote copies, remote signals or barrier semaphores. Data moves between devices by JAX's collectives and lax.ppermute only.
A program may use at most 192 MiB of HBM per device.

```python
import math
import jax
import jax.numpy as jnp
import numpy as np
from jax import lax

D = 6144
FFW = 5376
TOP = 4
TOK_OWN = 8
EXPERTS = 8
SUB = 1
HID_DEV = 2688
CAP = 5
TOKENS = 64
N_EXPERT = 8
N_BLK = 2


def block_scale(key, extent, shards, least, top_value):
    gain = 1.0
    for axis_at, shards_of in shards:
        heights = jax.random.uniform(jax.random.fold_in(jax.random.fold_in(key, 6), axis_at), (shards_of,), jnp.float32, least / len(shards), top_value / len(shards))
        gain = gain * jnp.repeat(jnp.exp(heights), extent[axis_at] // shards_of).reshape((-1,) + (1,) * (len(extent) - 1 - axis_at))
    return gain


def assign_block(stream_key, own, number, rows, amount, top, limit, slope):
    order = jax.random.permutation(stream_key, amount)
    crowded, ordinary = shares(amount, rows * top, limit, slope, True), shares(amount, rows * top, limit, slope, False)
    places = jnp.arange(amount)

    def named(sizes, offset_by):
        used = int((sizes > 0).sum())
        fixed = max(1, used // 4)
        moved = fixed + (places - fixed + offset_by * (used - fixed)) % max(1, amount - fixed)
        return jnp.zeros((amount,), jnp.int32).at[order[jnp.where(places < fixed, places, moved)]].set(jnp.asarray(sizes, jnp.int32))

    sizes = jnp.where(number % 4 == 0, named(crowded, number // 4), named(ordinary, number - number // 4 - 1))
    mixed = jax.random.permutation(jax.random.fold_in(own, 3), amount)
    donor, taker = mixed[0:amount // 2 * 2:2], mixed[1:amount // 2 * 2:2]
    slack = jnp.minimum(sizes[donor] - 1, limit - sizes[taker]) // 2
    slack = jnp.where((donor == order[0]) | (taker == order[0]) | (sizes[taker] == 0), 0, jnp.maximum(slack, 0))
    moved = jax.random.randint(jax.random.fold_in(own, 4), (amount // 2,), 0, 1 << 20) % (slack + 1)
    sizes = sizes.at[donor].add(-moved).at[taker].add(moved)
    items = jnp.searchsorted(jnp.cumsum(sizes), jnp.arange(rows * top), side="right").astype(jnp.int32)
    table = items.reshape(top, rows).T
    table = table[jax.random.permutation(jax.random.fold_in(own, 1), rows)]
    offset_by = jax.random.randint(jax.random.fold_in(own, 2), (rows, 1), 0, top)
    return jnp.take_along_axis(table, (jnp.arange(top)[None, :] + offset_by) % top, axis=1)


def shares(amount, total, reach, lean, full):
    loads = [(1 << 20) // math.isqrt(standing ** lean) + 1 for standing in range(1, amount + 1)]
    largest = reach if full else min(reach, max(-(-total // amount), total * loads[0] // sum(loads)))
    least = 1 if total - largest >= amount - 1 else 0
    holding, rest = [largest] + [least] * (amount - 1), total - largest - least * (amount - 1)
    while rest > 0:
        free = [i for i in range(1, amount) if holding[i] < largest] or [i for i in range(1, amount) if holding[i] < reach]
        whole, budget = sum([loads[i] for i in free]), rest
        for i in free:
            addition = min(reach - holding[i], max(1, budget * loads[i] // whole), rest)
            holding[i] = holding[i] + addition
            rest = rest - addition
    return np.array(holding)


def bell_draw(rng, extent, width, reach, cuts=(), kind=jnp.bfloat16):
    array = jax.random.normal(rng, extent, jnp.float32) * width
    if len(cuts) > 0:
        array = block_scale(rng, extent, cuts, -0.22, 0.18) * array
    return jnp.clip(array, min=-reach, max=reach).astype(kind)


def setup_inputs(seed: int = 0, part: int = 0) -> dict:
    streams_of = jax.random.split(jax.random.key(seed), 7)
    own_keys = jax.random.split(jax.random.fold_in(streams_of[6], part), 7)
    tokens = bell_draw(own_keys[0], (TOKENS, D), 1.0, 6.0, ((0, 8), (1, 2)))
    expert_ids_keys = jax.random.split(jax.random.fold_in(own_keys[1], 1), TOKENS // TOK_OWN)
    expert_ids_turns = jax.random.permutation(jax.random.fold_in(own_keys[1], 3), TOKENS // TOK_OWN)
    expert_ids = jax.vmap(lambda own, number: assign_block(jax.random.fold_in(own_keys[1], 2), own, number, TOK_OWN, EXPERTS, TOP, CAP, 2))(expert_ids_keys, expert_ids_turns).reshape((TOKENS, TOP))
    route_weight = jnp.clip(0.05 + 0.55 * jax.random.uniform(own_keys[2], (TOKENS, TOP), jnp.float32) ** block_scale(own_keys[2], (TOKENS, TOP), ((0, 8),), -0.2, 0.2), 0.05, 0.6)
    w_gate = bell_draw(streams_of[3], (N_EXPERT, FFW // SUB, D), D ** -0.5, 0.078125, ((0, 8), (1, 2)))
    w_up = bell_draw(streams_of[4], (N_EXPERT, FFW // SUB, D), D ** -0.5, 0.078125, ((0, 8), (1, 2)))
    w_down = bell_draw(streams_of[5], (N_EXPERT, FFW // SUB, D), FFW ** -0.5, 0.078125, ((0, 8), (1, 2)))
    return dict(tokens=tokens, expert_ids=expert_ids, route_weight=route_weight, w_gate=w_gate, w_up=w_up, w_down=w_down)


def reference(tokens, expert_ids, route_weight, w_gate, w_up, w_down):
    def shard_step(running, shard_id):
        gate_val = jnp.dot(tokens, w_gate[shard_id].T, preferred_element_type=jnp.float32)
        up_val = jnp.dot(tokens, w_up[shard_id].T, preferred_element_type=jnp.float32)
        hidden = (jax.nn.silu(gate_val) * up_val).astype(jnp.bfloat16)
        hidden_blocks = hidden.reshape(TOKENS, N_BLK, HID_DEV).astype(jnp.float32)
        down_blocks = w_down[shard_id].reshape(N_BLK, HID_DEV, D).astype(jnp.float32)
        pieces = jnp.einsum("tbh,bhf->btf", hidden_blocks, down_blocks)
        pieces = lax.optimization_barrier(pieces.astype(jnp.bfloat16)).astype(jnp.float32)
        block_out = jnp.sum(pieces, axis=0).astype(jnp.bfloat16)
        owner_expert = (shard_id // SUB).astype(jnp.int32)
        coef = jnp.sum(jnp.where(expert_ids == owner_expert, route_weight, jnp.float32(0.0)), axis=1)
        return running + coef[:, None] * block_out.astype(jnp.float32), None

    start_sum = jnp.zeros((TOKENS, D), jnp.float32)
    running, unused = lax.scan(shard_step, start_sum, jnp.arange(N_EXPERT, dtype=jnp.int32))
    return running.astype(jnp.bfloat16)
```

```python
import functools

import jax
import jax.numpy as jnp
from jax import lax
from jax.experimental import pallas as pl
from jax.experimental.pallas import tpu as pltpu
from jax.sharding import PartitionSpec as P

FFW = 5376
PAIR = 2
LANES = 128
SLOTS = 3
VMEM_LIMIT = 40 * 1024 * 1024
F32 = jnp.float32
BF16 = jnp.bfloat16


def dot_rows(left, right):
    return lax.dot_general(left, right, (((1,), (1,)), ((), ())), preferred_element_type=F32)


def largest_step(total, choices):
    for step in choices:
        if total % step == 0:
            return step
    return total


def call(kernel, outs, operands, spaces, scratch, flops, moved):
    return pl.pallas_call(
        kernel,
        out_shape=outs,
        in_specs=[pl.BlockSpec(memory_space=space) for space in spaces],
        out_specs=jax.tree.map(lambda unused: pl.BlockSpec(memory_space=pltpu.VMEM), outs),
        scratch_shapes=scratch,
        compiler_params=pltpu.CompilerParams(vmem_limit_bytes=VMEM_LIMIT),
        cost_estimate=pl.CostEstimate(flops=flops, bytes_accessed=moved, transcendentals=0),
    )(*operands)


def stream(count, copies, work):
    for step in range(min(SLOTS - 1, count)):
        for copy in copies(step, step):
            copy.start()

    def one(step, carry):
        slot = lax.rem(step, SLOTS)
        later = step + SLOTS - 1

        @pl.when(later < count)
        def _():
            for copy in copies(later, lax.rem(later, SLOTS)):
                copy.start()

        work(step, slot, copies(step, slot))
        return carry

    lax.fori_loop(0, count, one, 0)


def first_kernel(hb, own, other, w_gate, w_up, gate, up, x, gate_buf, up_buf, sems):
    half, width = own.shape[0], x.shape[1]
    x[:half] = own[:, :width]
    x[half:] = other[:, :width]
    column = pl.multiple_of(lax.axis_index("blk") * width, LANES)

    def copies(step, slot):
        rows = pl.ds(pl.multiple_of(step * hb, 8), hb)
        window = (0, rows, pl.ds(column, width))
        return (
            pltpu.make_async_copy(w_gate.at[window], gate_buf.at[slot], sems.at[0, slot]),
            pltpu.make_async_copy(w_up.at[window], up_buf.at[slot], sems.at[1, slot]),
        )

    def work(step, slot, waits):
        rows = pl.ds(pl.multiple_of(step * hb, 8), hb)
        waits[0].wait()
        gate[rows] = dot_rows(gate_buf[slot], x[...])
        waits[1].wait()
        up[rows] = dot_rows(up_buf[slot], x[...])

    stream(w_gate.shape[1] // hb, copies, work)


def second_kernel(hb, others, *refs):
    sent = refs[: 2 * others]
    gate, up, w_gate, w_up, hidden, x, gate_buf, up_buf, sems = refs[2 * others :]
    half, width = sent[0].shape
    for j in range(others):
        x[j, :half] = sent[2 * j][...]
        x[j, half:] = sent[2 * j + 1][...]
    here = lax.axis_index("blk")

    def copies(step, slot):
        rows = pl.ds(pl.multiple_of(step * hb, 8), hb)
        made = []
        for place, (weight, buf) in enumerate(((w_gate, gate_buf), (w_up, up_buf))):
            for j in range(others):
                column = pl.multiple_of(lax.rem(here + 1 + j, others + 1) * width, LANES)
                made.append(
                    pltpu.make_async_copy(
                        weight.at[0, rows, pl.ds(column, width)],
                        buf.at[slot, j],
                        sems.at[place, slot, j],
                    )
                )
        return made

    def work(step, slot, waits):
        rows = pl.ds(pl.multiple_of(step * hb, 8), hb)
        gate_acc, up_acc = gate[rows], up[rows]
        for j in range(others):
            waits[j].wait()
            gate_acc += dot_rows(gate_buf[slot, j], x[j])
        for j in range(others):
            waits[others + j].wait()
            up_acc += dot_rows(up_buf[slot, j], x[j])
        value = gate_acc / (1.0 + jnp.exp(-gate_acc)) * up_acc
        hidden[:, pl.ds(pl.multiple_of(step * hb, LANES), hb)] = value.T.astype(BF16)

    stream(w_gate.shape[1] // hb, copies, work)


def third_kernel(fb, parts, experts, shares, hidden, own, other, w_down, *refs):
    outs, (buf, sems) = refs[: 2 * len(parts)], refs[2 * len(parts) :]
    half, width = outs[0].shape
    steps = width // fb
    here, cycle = lax.axis_index("blk"), lax.axis_size("blk")
    expert = lax.axis_index("expert") // shares
    packed = jnp.concatenate([own[:, width:], other[:, width:]], axis=0).astype(F32)
    lane = lax.broadcasted_iota(jnp.int32, packed.shape, 1)
    mine = (lax.rem(lane, experts) == expert) & (lane < 3 * experts)
    coef = jnp.sum(jnp.where(mine, packed, 0.0), axis=1, keepdims=True)
    for place, part in enumerate(parts):
        first = lax.rem(here + part, cycle) * width

        def copies(step, slot):
            column = pl.multiple_of(first + step * fb, LANES)
            return (
                pltpu.make_async_copy(
                    w_down.at[0, :, pl.ds(column, fb)], buf.at[slot], sems.at[slot]
                ),
            )

        def work(step, slot, waits):
            waits[0].wait()
            value = jnp.dot(hidden[...], buf[slot], preferred_element_type=F32) * coef
            columns = pl.ds(pl.multiple_of(step * fb, LANES), fb)
            for at in range(2):
                out = outs[2 * place + at]
                out[:, columns] = value[at * half : (at + 1) * half].astype(out.dtype)

        stream(steps, copies, work)


def body(tokens, expert_ids, route_weight, w_gate, w_up, w_down):
    n_expert = lax.axis_size("expert")
    n_blk = lax.axis_size("blk")
    rows, width = tokens.shape
    hid, model = w_gate.shape[1:]
    shares = FFW // (hid * n_blk)
    experts = n_expert // shares
    places = n_expert // PAIR
    half = places * rows
    others = n_blk - 1

    chosen = expert_ids[:, :, None] == jnp.arange(experts, dtype=jnp.int32)[None, None, :]
    coef = jnp.sum(jnp.where(chosen, route_weight[:, :, None], 0.0), axis=1)
    high = lax.reduce_precision(coef, 8, 7)
    middle = lax.reduce_precision(coef - high, 8, 7)
    low = coef - high - middle
    table = jnp.concatenate([high, middle, low], axis=1).astype(BF16)
    room = -(-3 * experts // LANES) * LANES
    packed = jnp.concatenate([tokens, jnp.pad(table, ((0, 0), (0, room - 3 * experts)))], axis=1)

    def along(k):
        return [(s, ((s // PAIR + k) % places) * PAIR + s % PAIR) for s in range(n_expert)]

    def across(k):
        return [(s, (s + k) % n_blk) for s in range(n_blk)]

    def across_other(k):
        return [
            (s * n_blk + b, (s ^ 1) * n_blk + (b + k) % n_blk)
            for s in range(n_expert)
            for b in range(n_blk)
        ]

    swap = [(s, s ^ 1) for s in range(n_expert)]

    pieces = [packed] + [lax.ppermute(packed, "expert", along(k)) for k in range(1, places)]
    own = jnp.concatenate(pieces, axis=0)
    other = lax.ppermute(own, "expert", swap)
    bare = own[:, :width]
    sent = []
    for j in range(1, n_blk):
        sent.append(lax.ppermute(bare, "blk", across(-j)))
        sent.append(lax.ppermute(bare, ("expert", "blk"), across_other(-j)))

    hb = largest_step(hid, (384,))
    fb = largest_step(width, (512, 384, 256, 128))
    vmem, hbm = pltpu.VMEM, pl.ANY
    tokens_all = 2 * half
    gate, up = call(
        functools.partial(first_kernel, hb),
        [jax.ShapeDtypeStruct((hid, tokens_all), F32)] * 2,
        (own, other, w_gate, w_up),
        (vmem, vmem, hbm, hbm),
        [
            pltpu.VMEM((tokens_all, width), BF16),
            pltpu.VMEM((SLOTS, hb, width), BF16),
            pltpu.VMEM((SLOTS, hb, width), BF16),
            pltpu.SemaphoreType.DMA((2, SLOTS)),
        ],
        4 * tokens_all * hid * width,
        4 * hid * width,
    )
    hidden = call(
        functools.partial(second_kernel, hb, others),
        jax.ShapeDtypeStruct((tokens_all, hid), BF16),
        (*sent, gate, up, w_gate, w_up),
        (vmem,) * (len(sent) + 2) + (hbm, hbm),
        [
            pltpu.VMEM((others, tokens_all, width), BF16),
            pltpu.VMEM((SLOTS, others, hb, width), BF16),
            pltpu.VMEM((SLOTS, others, hb, width), BF16),
            pltpu.SemaphoreType.DMA((2, SLOTS, others)),
        ],
        4 * tokens_all * hid * width * others,
        4 * hid * width * others,
    )

    def down(parts, kinds):
        return call(
            functools.partial(third_kernel, fb, parts, experts, shares),
            [jax.ShapeDtypeStruct((half, width), kind) for unused in parts for kind in kinds],
            (hidden, own, other, w_down),
            (vmem, vmem, vmem, hbm),
            [pltpu.VMEM((SLOTS, hid, fb), BF16), pltpu.SemaphoreType.DMA((SLOTS,))],
            2 * tokens_all * hid * width * len(parts),
            2 * hid * width * len(parts),
        )

    away = down(tuple(range(1, n_blk)), (BF16, BF16))
    total = []
    for j in range(1, n_blk):
        total.append(lax.ppermute(away[2 * j - 2], "blk", across(j)))
        total.append(lax.ppermute(away[2 * j - 1], ("expert", "blk"), across_other(j)))
    kept, given = down((0,), (F32, BF16))
    total.append(lax.ppermute(given, "expert", swap))
    summed = kept
    for term in total:
        summed = summed + term.astype(F32)
    mixed = summed[:rows]
    for k in range(1, places):
        piece = summed[k * rows : (k + 1) * rows].astype(BF16)
        mixed = mixed + lax.ppermute(piece, "expert", along(-k)).astype(F32)
    return mixed.astype(BF16)


def solution(mesh):
    placed = (
        P(("groups", "expert"), "blk"),
        P(("groups", "expert"), None),
        P(("groups", "expert"), None),
        P("expert", "blk", None),
        P("expert", "blk", None),
        P("expert", "blk", None),
    )
    return jax.shard_map(
        body, mesh=mesh, in_specs=placed, out_specs=P(("groups", "expert"), "blk"), check_vma=False
    )
```

```python
import functools

import jax
import jax.numpy as jnp
from jax import lax
from jax.experimental import pallas as pl
from jax.experimental.pallas import tpu as pltpu
from jax.sharding import PartitionSpec as P

FFW = 5376
PAIR = 2
LANES = 128
SLOTS = 3
MIB = 1024 * 1024
F32 = jnp.float32
BF16 = jnp.bfloat16


def dot_rows(left, right):
    return lax.dot_general(left, right, (((1,), (1,)), ((), ())), preferred_element_type=F32)


def largest_step(total, choices):
    for step in choices:
        if total % step == 0:
            return step
    return total


def call(kernel, outs, operands, spaces, scratch, limit, flops, moved):
    return pl.pallas_call(
        kernel,
        out_shape=outs,
        in_specs=[pl.BlockSpec(memory_space=space) for space in spaces],
        out_specs=jax.tree.map(lambda unused: pl.BlockSpec(memory_space=pltpu.VMEM), outs),
        scratch_shapes=scratch,
        compiler_params=pltpu.CompilerParams(vmem_limit_bytes=limit * MIB),
        cost_estimate=pl.CostEstimate(flops=flops, bytes_accessed=moved, transcendentals=0),
    )(*operands)


def stream(count, copies, begin, work):
    for step in range(min(SLOTS - 1, count)):
        for copy in copies(step, step):
            copy.start()
    begin()

    def one(step, carry):
        slot = lax.rem(step, SLOTS)
        later = step + SLOTS - 1

        @pl.when(later < count)
        def _():
            for copy in copies(later, lax.rem(later, SLOTS)):
                copy.start()

        work(step, slot, copies(step, slot))
        return carry

    lax.fori_loop(0, count, one, 0)


def pack_kernel(experts, tokens, ids, weights, out):
    rows, width = tokens.shape
    out[:, :width] = tokens[...]
    shape = (rows, out.shape[1] - width)
    lane = lax.broadcasted_iota(jnp.int32, shape, 1)
    diagonal = lax.broadcasted_iota(jnp.int32, (rows, rows), 0) == lax.broadcasted_iota(
        jnp.int32, (rows, rows), 1
    )
    coef = jnp.zeros(shape, F32)
    for k in range(ids.shape[0]):
        name = jnp.sum(jnp.where(diagonal, ids[k : k + 1], 0), axis=1, keepdims=True)
        weight = jnp.sum(jnp.where(diagonal, weights[k : k + 1], 0.0), axis=1, keepdims=True)
        coef += jnp.where(lax.rem(lane, experts) == name, weight, 0.0)
    high = coef.astype(BF16).astype(F32)
    middle = (coef - high).astype(BF16).astype(F32)
    low = coef - high - middle
    part = jnp.where(lane < experts, high, jnp.where(lane < 2 * experts, middle, low))
    out[:, width:] = jnp.where(lane < 3 * experts, part, 0.0).astype(BF16)


def first_kernel(hb, own, other, w_gate, w_up, gate, up, x, gate_buf, up_buf, sems):
    half, width = own.shape[0], x.shape[1]
    column = pl.multiple_of(lax.axis_index("blk") * width, LANES)

    def copies(step, slot):
        rows = pl.ds(pl.multiple_of(step * hb, 8), hb)
        window = (0, rows, pl.ds(column, width))
        return (
            pltpu.make_async_copy(w_gate.at[window], gate_buf.at[slot], sems.at[0, slot]),
            pltpu.make_async_copy(w_up.at[window], up_buf.at[slot], sems.at[1, slot]),
        )

    def begin():
        x[:half] = own[:, :width]
        x[half:] = other[:, :width]

    def work(step, slot, waits):
        units = pl.ds(pl.multiple_of(step * hb, LANES), hb)
        waits[0].wait()
        gate[:, units] = dot_rows(x[...], gate_buf[slot])
        waits[1].wait()
        up[:, units] = dot_rows(x[...], up_buf[slot])

    stream(w_gate.shape[1] // hb, copies, begin, work)


def second_kernel(hb, others, *refs):
    sent = refs[: 2 * others]
    gate, up, w_gate, w_up, hidden, x, gate_buf, up_buf, sems = refs[2 * others :]
    half, width = sent[0].shape
    here = lax.axis_index("blk")

    def copies(step, slot):
        rows = pl.ds(pl.multiple_of(step * hb, 8), hb)
        made = []
        for place, (weight, buf) in enumerate(((w_gate, gate_buf), (w_up, up_buf))):
            for j in range(others):
                column = pl.multiple_of(lax.rem(here + 1 + j, others + 1) * width, LANES)
                made.append(
                    pltpu.make_async_copy(
                        weight.at[0, rows, pl.ds(column, width)],
                        buf.at[slot, j],
                        sems.at[place, slot, j],
                    )
                )
        return made

    def begin():
        for j in range(others):
            x[j, :half] = sent[2 * j][...]
            x[j, half:] = sent[2 * j + 1][...]

    def work(step, slot, waits):
        units = pl.ds(pl.multiple_of(step * hb, LANES), hb)
        gate_acc, up_acc = gate[:, units], up[:, units]
        for j in range(others):
            waits[j].wait()
            gate_acc += dot_rows(x[j], gate_buf[slot, j])
        for j in range(others):
            waits[others + j].wait()
            up_acc += dot_rows(x[j], up_buf[slot, j])
        value = gate_acc / (1.0 + jnp.exp(-gate_acc)) * up_acc
        hidden[:, units] = value.astype(BF16)

    stream(w_gate.shape[1] // hb, copies, begin, work)


def third_kernel(fb, parts, experts, shares, hidden, own, other, w_down, *refs):
    outs, (buf, sems) = refs[: 2 * len(parts)], refs[2 * len(parts) :]
    half, width = outs[0].shape
    steps = width // fb
    here, cycle = lax.axis_index("blk"), lax.axis_size("blk")
    expert = lax.axis_index("expert") // shares
    packed = jnp.concatenate([own[:, width:], other[:, width:]], axis=0).astype(F32)
    lane = lax.broadcasted_iota(jnp.int32, packed.shape, 1)
    mine = (lax.rem(lane, experts) == expert) & (lane < 3 * experts)
    coef = jnp.sum(jnp.where(mine, packed, 0.0), axis=1, keepdims=True)
    for place, part in enumerate(parts):
        first = lax.rem(here + part, cycle) * width

        def copies(step, slot):
            column = pl.multiple_of(first + step * fb, LANES)
            return (
                pltpu.make_async_copy(
                    w_down.at[0, :, pl.ds(column, fb)], buf.at[slot], sems.at[slot]
                ),
            )

        def work(step, slot, waits):
            waits[0].wait()
            value = jnp.dot(hidden[...], buf[slot], preferred_element_type=F32) * coef
            columns = pl.ds(pl.multiple_of(step * fb, LANES), fb)
            for at in range(2):
                out = outs[2 * place + at]
                out[:, columns] = value[at * half : (at + 1) * half].astype(out.dtype)

        stream(steps, copies, lambda: None, work)


def body(tokens, expert_ids, route_weight, w_gate, w_up, w_down):
    n_expert = lax.axis_size("expert")
    n_blk = lax.axis_size("blk")
    rows, width = tokens.shape
    hid, model = w_gate.shape[1:]
    shares = FFW // (hid * n_blk)
    experts = n_expert // shares
    places = n_expert // PAIR
    half = places * rows
    others = n_blk - 1

    room = -(-3 * experts // LANES) * LANES
    vmem, hbm = pltpu.VMEM, pl.ANY
    packed = call(
        functools.partial(pack_kernel, experts),
        jax.ShapeDtypeStruct((rows, width + room), BF16),
        (tokens, expert_ids.T, route_weight.T),
        (vmem,) * 3,
        [],
        8,
        rows * room,
        4 * rows * width,
    )

    def along(k):
        return [(s, ((s // PAIR + k) % places) * PAIR + s % PAIR) for s in range(n_expert)]

    def across(k):
        return [(s, (s + k) % n_blk) for s in range(n_blk)]

    def across_other(k):
        return [
            (s * n_blk + b, (s ^ 1) * n_blk + (b + k) % n_blk)
            for s in range(n_expert)
            for b in range(n_blk)
        ]

    swap = [(s, s ^ 1) for s in range(n_expert)]

    pieces = [packed] + [lax.ppermute(packed, "expert", along(k)) for k in range(1, places)]
    own = jnp.concatenate(pieces, axis=0)
    other = lax.ppermute(own, "expert", swap)
    bare = own[:, :width]
    sent = []
    for j in range(1, n_blk):
        sent.append(lax.ppermute(bare, "blk", across(-j)))
        sent.append(lax.ppermute(bare, ("expert", "blk"), across_other(-j)))

    hb = largest_step(hid, (384,))
    fb = largest_step(width, (512, 384, 256, 128))
    tokens_all = 2 * half
    w_gate = pltpu.with_memory_space_constraint(w_gate, pltpu.HBM)
    w_up = pltpu.with_memory_space_constraint(w_up, pltpu.HBM)
    w_down = pltpu.with_memory_space_constraint(w_down, pltpu.HBM)
    gate, up = call(
        functools.partial(first_kernel, hb),
        [jax.ShapeDtypeStruct((tokens_all, hid), F32)] * 2,
        (own, other, w_gate, w_up),
        (vmem, vmem, hbm, hbm),
        [
            pltpu.VMEM((tokens_all, width), BF16),
            pltpu.VMEM((SLOTS, hb, width), BF16),
            pltpu.VMEM((SLOTS, hb, width), BF16),
            pltpu.SemaphoreType.DMA((2, SLOTS)),
        ],
        24,
        4 * tokens_all * hid * width,
        4 * hid * width,
    )
    hidden = call(
        functools.partial(second_kernel, hb, others),
        jax.ShapeDtypeStruct((tokens_all, hid), BF16),
        (*sent, gate, up, w_gate, w_up),
        (vmem,) * (len(sent) + 2) + (hbm, hbm),
        [
            pltpu.VMEM((others, tokens_all, width), BF16),
            pltpu.VMEM((SLOTS, others, hb, width), BF16),
            pltpu.VMEM((SLOTS, others, hb, width), BF16),
            pltpu.SemaphoreType.DMA((2, SLOTS, others)),
        ],
        24,
        4 * tokens_all * hid * width * others,
        4 * hid * width * others,
    )

    def down(parts, kinds):
        return call(
            functools.partial(third_kernel, fb, parts, experts, shares),
            [jax.ShapeDtypeStruct((half, width), kind) for unused in parts for kind in kinds],
            (hidden, own, other, w_down),
            (vmem, vmem, vmem, hbm),
            [pltpu.VMEM((SLOTS, hid, fb), BF16), pltpu.SemaphoreType.DMA((SLOTS,))],
            20,
            2 * tokens_all * hid * width * len(parts),
            2 * hid * width * len(parts),
        )

    away = down(tuple(range(1, n_blk)), (BF16, BF16))
    total = []
    for j in range(1, n_blk):
        total.append(lax.ppermute(away[2 * j - 2], "blk", across(j)))
        total.append(lax.ppermute(away[2 * j - 1], ("expert", "blk"), across_other(j)))
    kept, given = down((0,), (F32, BF16))
    total.append(lax.ppermute(given, "expert", swap))
    summed = kept
    for term in total:
        summed = summed + term.astype(F32)
    mixed = summed[:rows]
    for k in range(1, places):
        piece = summed[k * rows : (k + 1) * rows].astype(BF16)
        mixed = mixed + lax.ppermute(piece, "expert", along(-k)).astype(F32)
    return mixed.astype(BF16)


def solution(mesh):
    placed = (
        P(("groups", "expert"), "blk"),
        P(("groups", "expert"), None),
        P(("groups", "expert"), None),
        P("expert", "blk", None),
        P("expert", "blk", None),
        P("expert", "blk", None),
    )
    return jax.shard_map(
        body, mesh=mesh, in_specs=placed, out_specs=P(("groups", "expert"), "blk"), check_vma=False
    )
```

```python
import functools

import jax
import jax.numpy as jnp
from jax import lax
from jax.experimental import pallas as pl
from jax.experimental.pallas import tpu as pltpu
from jax.sharding import PartitionSpec as P

FFW = 5376
PAIR = 2
LANES = 128
SLOTS = 3
MIB = 1024 * 1024
F32 = jnp.float32
BF16 = jnp.bfloat16


def dot_rows(left, right):
    return lax.dot_general(left, right, (((1,), (1,)), ((), ())), preferred_element_type=F32)


def largest_step(total, choices):
    for step in choices:
        if total % step == 0:
            return step
    return total


def call(kernel, outs, operands, spaces, scratch, limit, flops, moved):
    return pl.pallas_call(
        kernel,
        out_shape=outs,
        in_specs=[pl.BlockSpec(memory_space=space) for space in spaces],
        out_specs=jax.tree.map(lambda unused: pl.BlockSpec(memory_space=pltpu.VMEM), outs),
        scratch_shapes=scratch,
        compiler_params=pltpu.CompilerParams(vmem_limit_bytes=limit * MIB),
        cost_estimate=pl.CostEstimate(flops=flops, bytes_accessed=moved, transcendentals=0),
    )(*operands)


def in_hbm(*arrays):
    return [pltpu.with_memory_space_constraint(array, pltpu.HBM) for array in arrays]


def stream(count, copies, begin, work):
    for step in range(min(SLOTS - 1, count)):
        for copy in copies(step, step):
            copy.start()
    begin()

    def one(step, carry):
        slot = lax.rem(step, SLOTS)
        later = step + SLOTS - 1

        @pl.when(later < count)
        def _():
            for copy in copies(later, lax.rem(later, SLOTS)):
                copy.start()

        work(step, slot, copies(step, slot))
        return carry

    lax.fori_loop(0, count, one, 0)


def pack_kernel(experts, tokens, ids, weights, out, held, named, weighed, sems):
    moves = [
        pltpu.make_async_copy(source, target, sems.at[at])
        for at, (source, target) in enumerate(((ids, named), (weights, weighed), (tokens, held)))
    ]
    for move in moves:
        move.start()
    rows, width = tokens.shape
    shape = (rows, out.shape[1] - width)
    lane = lax.broadcasted_iota(jnp.int32, shape, 1)
    diagonal = lax.broadcasted_iota(jnp.int32, (rows, rows), 0) == lax.broadcasted_iota(
        jnp.int32, (rows, rows), 1
    )
    coef = jnp.zeros(shape, F32)
    moves[0].wait()
    moves[1].wait()
    for k in range(ids.shape[0]):
        name = jnp.sum(jnp.where(diagonal, named[k : k + 1], 0), axis=1, keepdims=True)
        weight = jnp.sum(jnp.where(diagonal, weighed[k : k + 1], 0.0), axis=1, keepdims=True)
        coef += jnp.where(lax.rem(lane, experts) == name, weight, 0.0)
    high = coef.astype(BF16).astype(F32)
    middle = (coef - high).astype(BF16).astype(F32)
    low = coef - high - middle
    part = jnp.where(lane < experts, high, jnp.where(lane < 2 * experts, middle, low))
    out[:, width:] = jnp.where(lane < 3 * experts, part, 0.0).astype(BF16)
    moves[2].wait()
    out[:, :width] = held[...]


def up_kernel(hb, rows, width, experts, shares, gathered, w_gate, w_up, *refs):
    hidden, coef_out, x, zero, gate_buf, up_buf, sems = refs
    n_blk, tokens_all = x.shape[:2]
    device, n_expert = lax.axis_index("expert"), lax.axis_size("expert")
    places = n_expert // PAIR
    chunk = gathered.shape[1] // (n_expert * n_blk)

    def copies(step, slot):
        units = pl.ds(pl.multiple_of(step * hb, 8), hb)
        return [
            pltpu.make_async_copy(
                weight.at[0, units, pl.ds(j * width, width)],
                buf.at[slot, j],
                sems.at[place, slot, j],
            )
            for place, (weight, buf) in enumerate(((w_gate, gate_buf), (w_up, up_buf)))
            for j in range(n_blk)
        ]

    def owned(j, column, size):
        pieces = []
        for other in range(PAIR):
            core = lax.rem(device + other, PAIR)
            for k in range(places):
                place = lax.rem(device // PAIR + places - k, places)
                first = ((place * PAIR + core) * n_blk + j) * chunk + column
                pieces.append(gathered[:, pl.ds(pl.multiple_of(first, LANES), size)])
        return jnp.concatenate(pieces, axis=0)

    def begin():
        for j in range(n_blk):
            x[j] = owned(j, 0, width)
        packed = owned(0, width, chunk - width).astype(F32)
        lane = lax.broadcasted_iota(jnp.int32, packed.shape, 1)
        mine = (lax.rem(lane, experts) == device // shares) & (lane < 3 * experts)
        coef = jnp.sum(jnp.where(mine, packed, 0.0), axis=1, keepdims=True)
        coef_out[...] = jnp.broadcast_to(coef, coef_out.shape)
        zero[...] = jnp.zeros_like(zero)

    def work(step, slot, waits):
        gate_acc = up_acc = zero[...]
        for j in range(n_blk):
            waits[j].wait()
            gate_acc += dot_rows(gate_buf[slot, j], x[j])
        for j in range(n_blk):
            waits[n_blk + j].wait()
            up_acc += dot_rows(up_buf[slot, j], x[j])
        value = gate_acc / (1.0 + jnp.exp(-gate_acc)) * up_acc
        hidden[:, pl.ds(pl.multiple_of(step * hb, LANES), hb)] = value.T.astype(BF16)

    stream(w_gate.shape[1] // hb, copies, begin, work)


def down_kernel(fb, parts, hidden, coef, w_down, *refs):
    outs, (buf, sems) = refs[: len(parts)], refs[len(parts) :]
    width = outs[0].shape[1]
    here, cycle = lax.axis_index("blk"), lax.axis_size("blk")
    for part, out in zip(parts, outs):
        first = lax.rem(here + part, cycle) * width

        def copies(step, slot):
            columns = pl.ds(pl.multiple_of(first + step * fb, LANES), fb)
            return [pltpu.make_async_copy(w_down.at[0, :, columns], buf.at[slot], sems.at[slot])]

        def work(step, slot, waits):
            waits[0].wait()
            value = jnp.dot(hidden[...], buf[slot], preferred_element_type=F32) * coef[:, :1]
            columns = pl.ds(pl.multiple_of(step * fb, LANES), fb)
            out[:, columns] = value.astype(out.dtype)

        stream(width // fb, copies, lambda: None, work)


def body(tokens, expert_ids, route_weight, w_gate, w_up, w_down):
    n_expert = lax.axis_size("expert")
    n_blk = lax.axis_size("blk")
    rows, width = tokens.shape
    top = expert_ids.shape[1]
    hid, model = w_gate.shape[1:]
    shares = FFW // (hid * n_blk)
    experts = n_expert // shares
    places = n_expert // PAIR
    half = places * rows
    tokens_all = PAIR * half
    room = -(-3 * experts // LANES) * LANES
    vmem, hbm = pltpu.VMEM, pl.ANY
    w_gate, w_up, w_down = in_hbm(w_gate, w_up, w_down)

    packed = call(
        functools.partial(pack_kernel, experts),
        jax.ShapeDtypeStruct((rows, width + room), BF16),
        in_hbm(tokens, expert_ids.T, route_weight.T),
        (hbm,) * 3,
        [
            pltpu.VMEM((rows, width), BF16),
            pltpu.VMEM((top, rows), jnp.int32),
            pltpu.VMEM((top, rows), F32),
            pltpu.SemaphoreType.DMA((3,)),
        ],
        8,
        rows * room,
        4 * rows * width,
    )
    gathered = lax.all_gather(packed, ("expert", "blk"), axis=1, tiled=True)

    hb = largest_step(hid, (384,))
    hidden, coef = call(
        functools.partial(up_kernel, hb, rows, width, experts, shares),
        [
            jax.ShapeDtypeStruct((tokens_all, hid), BF16),
            jax.ShapeDtypeStruct((tokens_all, LANES), F32),
        ],
        (gathered, w_gate, w_up),
        (vmem, hbm, hbm),
        [
            pltpu.VMEM((n_blk, tokens_all, width), BF16),
            pltpu.VMEM((hb, tokens_all), F32),
            pltpu.VMEM((SLOTS, n_blk, hb, width), BF16),
            pltpu.VMEM((SLOTS, n_blk, hb, width), BF16),
            pltpu.SemaphoreType.DMA((2, SLOTS, n_blk)),
        ],
        40,
        4 * tokens_all * hid * model,
        4 * hid * model,
    )

    fb = largest_step(width, (512, 384, 256, 128))

    def down(parts, kind):
        return call(
            functools.partial(down_kernel, fb, parts),
            [jax.ShapeDtypeStruct((tokens_all, width), kind) for unused in parts],
            (hidden, coef, w_down),
            (vmem, vmem, hbm),
            [pltpu.VMEM((SLOTS, hid, fb), BF16), pltpu.SemaphoreType.DMA((SLOTS,))],
            20,
            2 * tokens_all * hid * width * len(parts),
            2 * hid * width * len(parts),
        )

    def along(k):
        return [(s, ((s // PAIR + k) % places) * PAIR + s % PAIR) for s in range(n_expert)]

    away = down(tuple(range(1, n_blk)), BF16)
    came = [
        lax.ppermute(part, "blk", [(s, (s + j) % n_blk) for s in range(n_blk)])
        for j, part in enumerate(away, 1)
    ]
    (summed,) = down((0,), F32)
    for part in came:
        summed = summed + part.astype(F32)
    given = lax.ppermute(
        summed[half:].astype(BF16), "expert", [(s, s ^ 1) for s in range(n_expert)]
    )
    summed = summed[:half] + given.astype(F32)
    mixed = summed[:rows]
    for k in range(1, places):
        piece = summed[k * rows : (k + 1) * rows].astype(BF16)
        mixed = mixed + lax.ppermute(piece, "expert", along(-k)).astype(F32)
    return mixed.astype(BF16)


def solution(mesh):
    placed = (
        P(("groups", "expert"), "blk"),
        P(("groups", "expert"), None),
        P(("groups", "expert"), None),
        P("expert", "blk", None),
        P("expert", "blk", None),
        P("expert", "blk", None),
    )
    return jax.shard_map(
        body, mesh=mesh, in_specs=placed, out_specs=P(("groups", "expert"), "blk"), check_vma=False
    )
```

```python
import functools

import jax
import jax.numpy as jnp
from jax import lax
from jax.experimental import pallas as pl
from jax.experimental.pallas import tpu as pltpu
from jax.sharding import PartitionSpec as P

FFW = 5376
PAIR = 2
LANES = 128
SLOTS = 3
MIB = 1024 * 1024
F32 = jnp.float32
BF16 = jnp.bfloat16


def largest_step(total, choices):
    for step in choices:
        if total % step == 0:
            return step
    return total


def call(kernel, outs, operands, spaces, scratch, limit, flops, moved):
    return pl.pallas_call(
        kernel,
        out_shape=outs,
        in_specs=[pl.BlockSpec(memory_space=space) for space in spaces],
        out_specs=jax.tree.map(lambda unused: pl.BlockSpec(memory_space=pltpu.VMEM), outs),
        scratch_shapes=scratch,
        compiler_params=pltpu.CompilerParams(vmem_limit_bytes=limit * MIB),
        cost_estimate=pl.CostEstimate(flops=flops, bytes_accessed=moved, transcendentals=0),
    )(*operands)


def in_hbm(*arrays):
    return [pltpu.with_memory_space_constraint(array, pltpu.HBM) for array in arrays]


def stream(count, copies, begin, work):
    for step in range(min(SLOTS - 1, count)):
        for copy in copies(step, step):
            copy.start()
    begin()

    def one(step, carry):
        slot = lax.rem(step, SLOTS)
        later = step + SLOTS - 1

        @pl.when(later < count)
        def _():
            for copy in copies(later, lax.rem(later, SLOTS)):
                copy.start()

        work(step, slot, copies(step, slot))
        return carry

    lax.fori_loop(0, count, one, 0)


def pack_kernel(experts, tokens, ids, weights, out, held, named, weighed, sems):
    moves = [
        pltpu.make_async_copy(source, target, sems.at[at])
        for at, (source, target) in enumerate(((ids, named), (weights, weighed), (tokens, held)))
    ]
    for move in moves:
        move.start()
    rows, width = tokens.shape
    shape = (rows, out.shape[1] - width)
    lane = lax.broadcasted_iota(jnp.int32, shape, 1)
    diagonal = lax.broadcasted_iota(jnp.int32, (rows, rows), 0) == lax.broadcasted_iota(
        jnp.int32, (rows, rows), 1
    )
    coef = jnp.zeros(shape, F32)
    moves[0].wait()
    moves[1].wait()
    for k in range(ids.shape[0]):
        name = jnp.sum(jnp.where(diagonal, named[k : k + 1], 0), axis=1, keepdims=True)
        weight = jnp.sum(jnp.where(diagonal, weighed[k : k + 1], 0.0), axis=1, keepdims=True)
        coef += jnp.where(lax.rem(lane, experts) == name, weight, 0.0)
    high = coef.astype(BF16).astype(F32)
    middle = (coef - high).astype(BF16).astype(F32)
    low = coef - high - middle
    part = jnp.where(lane < experts, high, jnp.where(lane < 2 * experts, middle, low))
    out[:, width:] = jnp.where(lane < 3 * experts, part, 0.0).astype(BF16)
    moves[2].wait()
    out[:, :width] = held[...]


def up_kernel(kb, parts, last, *refs):
    sent, refs = refs[: 2 * len(parts)], refs[2 * len(parts) :]
    held, refs = (refs[:2], refs[2:]) if last else ((), refs)
    w_gate, w_up = refs[:2]
    outs, (x, gate_buf, up_buf, sems, *sums) = (refs[2:3], refs[3:]) if last else (refs[2:4], refs[4:])
    gate_sum, up_sum = sums if last else outs
    half, hid = sent[0].shape[0], w_gate.shape[1]
    width = x.shape[0] // len(parts)
    per = width // kb
    here, cycle = lax.axis_index("blk"), lax.axis_size("blk")

    def copies(step, slot):
        owner = lax.rem(here + parts[0] + step // per, cycle)
        columns = pl.ds(pl.multiple_of(owner * width + lax.rem(step, per) * kb, LANES), kb)
        return [
            pltpu.make_async_copy(w_gate.at[0, :, columns], gate_buf.at[slot], sems.at[0, slot]),
            pltpu.make_async_copy(w_up.at[0, :, columns], up_buf.at[slot], sems.at[1, slot]),
        ]

    def begin():
        for j in range(len(parts)):
            rows = [sent[2 * j + at][:, :width].astype(F32) for at in range(2)]
            x[j * width : (j + 1) * width] = jnp.concatenate(rows, axis=0).T.astype(BF16)
        gate_sum[...] = held[0][...] if last else jnp.zeros_like(gate_sum)
        up_sum[...] = held[1][...] if last else jnp.zeros_like(up_sum)

    def work(step, slot, waits):
        right = x[pl.ds(pl.multiple_of(step * kb, LANES), kb)]
        waits[0].wait()
        gate_sum[...] += jnp.dot(gate_buf[slot], right, preferred_element_type=F32)
        waits[1].wait()
        up_sum[...] += jnp.dot(up_buf[slot], right, preferred_element_type=F32)

    stream(len(parts) * per, copies, begin, work)
    if last:
        unit = largest_step(hid, (384,))
        for first in range(0, hid, unit):
            units = pl.ds(first, unit)
            gate = gate_sum[units]
            value = gate / (1.0 + jnp.exp(-gate)) * up_sum[units]
            outs[0][:, units] = value.T.astype(BF16)


def down_kernel(fb, parts, experts, shares, hidden, own, other, w_down, *refs):
    outs, (buf, sems) = refs[: 2 * len(parts)], refs[2 * len(parts) :]
    half, width = outs[0].shape
    here, cycle = lax.axis_index("blk"), lax.axis_size("blk")
    expert = lax.axis_index("expert") // shares
    packed = jnp.concatenate([own[:, width:], other[:, width:]], axis=0).astype(F32)
    lane = lax.broadcasted_iota(jnp.int32, packed.shape, 1)
    mine = (lax.rem(lane, experts) == expert) & (lane < 3 * experts)
    coef = jnp.sum(jnp.where(mine, packed, 0.0), axis=1, keepdims=True)
    for place, part in enumerate(parts):
        first = lax.rem(here + part, cycle) * width

        def copies(step, slot):
            columns = pl.ds(pl.multiple_of(first + step * fb, LANES), fb)
            return [pltpu.make_async_copy(w_down.at[0, :, columns], buf.at[slot], sems.at[slot])]

        def work(step, slot, waits):
            waits[0].wait()
            value = jnp.dot(hidden[...], buf[slot], preferred_element_type=F32) * coef
            columns = pl.ds(pl.multiple_of(step * fb, LANES), fb)
            for at in range(2):
                out = outs[2 * place + at]
                out[:, columns] = value[at * half : (at + 1) * half].astype(out.dtype)

        stream(width // fb, copies, lambda: None, work)


def body(tokens, expert_ids, route_weight, w_gate, w_up, w_down):
    n_expert = lax.axis_size("expert")
    n_blk = lax.axis_size("blk")
    rows, width = tokens.shape
    top = expert_ids.shape[1]
    hid = w_gate.shape[1]
    shares = FFW // (hid * n_blk)
    experts = n_expert // shares
    places = n_expert // PAIR
    half = places * rows
    tokens_all = PAIR * half
    room = -(-3 * experts // LANES) * LANES
    vmem, hbm = pltpu.VMEM, pl.ANY
    w_gate, w_up, w_down = in_hbm(w_gate, w_up, w_down)

    packed = call(
        functools.partial(pack_kernel, experts),
        jax.ShapeDtypeStruct((rows, width + room), BF16),
        in_hbm(tokens, expert_ids.T, route_weight.T),
        (hbm,) * 3,
        [
            pltpu.VMEM((rows, width), BF16),
            pltpu.VMEM((top, rows), jnp.int32),
            pltpu.VMEM((top, rows), F32),
            pltpu.SemaphoreType.DMA((3,)),
        ],
        8,
        rows * room,
        4 * rows * width,
    )

    def along(k):
        return [(s, ((s // PAIR + k) % places) * PAIR + s % PAIR) for s in range(n_expert)]

    def across(k):
        return [(s, (s + k) % n_blk) for s in range(n_blk)]

    def across_other(k):
        return [
            (s * n_blk + b, (s ^ 1) * n_blk + (b + k) % n_blk)
            for s in range(n_expert)
            for b in range(n_blk)
        ]

    swap = [(s, s ^ 1) for s in range(n_expert)]

    pieces = [packed] + [lax.ppermute(packed, "expert", along(k)) for k in range(1, places)]
    own = jnp.concatenate(pieces, axis=0)
    other = lax.ppermute(own, "expert", swap)
    bare = own[:, :width]
    sent = []
    for j in range(1, n_blk):
        sent.append(lax.ppermute(bare, "blk", across(-j)))
        sent.append(lax.ppermute(bare, ("expert", "blk"), across_other(-j)))

    kb = largest_step(width, (512, 384, 256, 128))
    sums = [jax.ShapeDtypeStruct((hid, tokens_all), F32)] * 2

    def up(parts, last, outs, operands):
        return call(
            functools.partial(up_kernel, kb, parts, last),
            outs,
            (*operands, w_gate, w_up),
            (vmem,) * len(operands) + (hbm, hbm),
            [
                pltpu.VMEM((width * len(parts), tokens_all), BF16),
                pltpu.VMEM((SLOTS, hid, kb), BF16),
                pltpu.VMEM((SLOTS, hid, kb), BF16),
                pltpu.SemaphoreType.DMA((2, SLOTS)),
            ]
            + [pltpu.VMEM(each.shape, F32) for each in sums if last],
            32,
            4 * tokens_all * hid * width * len(parts),
            4 * hid * width * len(parts),
        )

    partial_sums = up((0,), False, sums, (own, other))
    hidden = up(
        tuple(range(1, n_blk)),
        True,
        jax.ShapeDtypeStruct((tokens_all, hid), BF16),
        (*sent, *partial_sums),
    )

    fb = largest_step(width, (512, 384, 256, 128))

    def down(parts, kinds):
        return call(
            functools.partial(down_kernel, fb, parts, experts, shares),
            [jax.ShapeDtypeStruct((half, width), kind) for unused in parts for kind in kinds],
            (hidden, own, other, w_down),
            (vmem, vmem, vmem, hbm),
            [pltpu.VMEM((SLOTS, hid, fb), BF16), pltpu.SemaphoreType.DMA((SLOTS,))],
            20,
            2 * tokens_all * hid * width * len(parts),
            2 * hid * width * len(parts),
        )

    away = down(tuple(range(1, n_blk)), (BF16, BF16))
    total = []
    for j in range(1, n_blk):
        total.append(lax.ppermute(away[2 * j - 2], "blk", across(j)))
        total.append(lax.ppermute(away[2 * j - 1], ("expert", "blk"), across_other(j)))
    kept, given = down((0,), (F32, BF16))
    total.append(lax.ppermute(given, "expert", swap))
    summed = kept
    for term in total:
        summed = summed + term.astype(F32)
    mixed = summed[:rows]
    for k in range(1, places):
        piece = summed[k * rows : (k + 1) * rows].astype(BF16)
        mixed = mixed + lax.ppermute(piece, "expert", along(-k)).astype(F32)
    return mixed.astype(BF16)


def solution(mesh):
    placed = (
        P(("groups", "expert"), "blk"),
        P(("groups", "expert"), None),
        P(("groups", "expert"), None),
        P("expert", "blk", None),
        P("expert", "blk", None),
        P("expert", "blk", None),
    )
    return jax.shard_map(
        body, mesh=mesh, in_specs=placed, out_specs=P(("groups", "expert"), "blk"), check_vma=False
    )
```

```python
import functools

import jax
import jax.numpy as jnp
from jax import lax
from jax.experimental import pallas as pl
from jax.experimental.pallas import tpu as pltpu
from jax.sharding import PartitionSpec as P

FFW = 5376
PAIR = 2
LANES = 128
SLOTS = 3
MIB = 1024 * 1024
F32 = jnp.float32
BF16 = jnp.bfloat16


def largest_step(total, choices):
    for step in choices:
        if total % step == 0:
            return step
    return total


def call(kernel, outs, operands, spaces, scratch, limit, flops, moved):
    return pl.pallas_call(
        kernel,
        out_shape=outs,
        in_specs=[pl.BlockSpec(memory_space=space) for space in spaces],
        out_specs=[pl.BlockSpec(memory_space=pltpu.VMEM) for unused in outs],
        scratch_shapes=scratch,
        compiler_params=pltpu.CompilerParams(vmem_limit_bytes=limit * MIB),
        cost_estimate=pl.CostEstimate(flops=flops, bytes_accessed=moved, transcendentals=0),
    )(*operands)


def in_hbm(*arrays):
    return [pltpu.with_memory_space_constraint(array, pltpu.HBM) for array in arrays]


def columns_of(step, per, block):
    owner = lax.rem(lax.axis_index("blk") + step // per, lax.axis_size("blk"))
    return pl.ds(pl.multiple_of((owner * per + lax.rem(step, per)) * block, LANES), block)


def moves(weights, step, per, targets, sems):
    return [
        pltpu.make_async_copy(weight.at[0, :, columns_of(step, per, target.shape[-1])], target, sem)
        for weight, target, sem in zip(weights, targets, sems)
    ]


def stream(held, count, fetch, ahead, begin, from_held, from_ring):
    rest = count - held
    for at in range(min(SLOTS, rest)):
        for copy in fetch(held + at, at):
            copy.start()
    if rest == 0:
        for copy in ahead:
            copy.start()
    begin()

    def first(step, carry):
        from_held(step)
        return carry

    if held:
        lax.fori_loop(0, held, first, 0)

    def then(at, carry):
        later = at + SLOTS - 1

        @pl.when((at > 0) & (later < rest))
        def _():
            for copy in fetch(held + later, lax.rem(later, SLOTS)):
                copy.start()

        @pl.when(at == max(rest - SLOTS, 0))
        def _():
            for copy in ahead:
                copy.start()

        slot = lax.rem(at, SLOTS)
        from_ring(held + at, slot, fetch(held + at, slot))
        return carry

    if rest:
        lax.fori_loop(0, rest, then, 0)


def finish(copies):
    for copy in copies:
        copy.wait()


def head_kernel(count, per, after, w_gate, w_up, gate, up, sems):
    copies = []
    for step in range(count):
        at = (sems.at[0, step], sems.at[1, step])
        copies += moves((w_gate, w_up), step, per, (gate.at[step], up.at[step]), at)
    for copy in copies:
        copy.start()
    finish(copies)


def pack_kernel(experts, tokens, ids, weights, out, held, named, weighed, sems):
    copies = [
        pltpu.make_async_copy(source, target, sems.at[at])
        for at, (source, target) in enumerate(((ids, named), (weights, weighed), (tokens, held)))
    ]
    for copy in copies:
        copy.start()
    rows, width = tokens.shape
    shape = (rows, out.shape[1] - width)
    lane = lax.broadcasted_iota(jnp.int32, shape, 1)
    diagonal = lax.broadcasted_iota(jnp.int32, (rows, rows), 0) == lax.broadcasted_iota(
        jnp.int32, (rows, rows), 1
    )
    coef = jnp.zeros(shape, F32)
    copies[0].wait()
    copies[1].wait()
    for k in range(ids.shape[0]):
        name = jnp.sum(jnp.where(diagonal, named[k : k + 1], 0), axis=1, keepdims=True)
        weight = jnp.sum(jnp.where(diagonal, weighed[k : k + 1], 0.0), axis=1, keepdims=True)
        coef += jnp.where(lax.rem(lane, experts) == name, weight, 0.0)
    high = coef.astype(BF16).astype(F32)
    middle = (coef - high).astype(BF16).astype(F32)
    low = coef - high - middle
    part = jnp.where(lane < experts, high, jnp.where(lane < 2 * experts, middle, low))
    out[:, width:] = jnp.where(lane < 3 * experts, part, 0.0).astype(BF16)
    copies[2].wait()
    out[:, :width] = held[...]


def up_kernel(kb, parts, held, more, last, *refs):
    sent, refs = refs[: 2 * len(parts)], refs[2 * len(parts) :]
    earlier, refs = (refs[:2], refs[2:]) if last else ((), refs)
    (gate_held, up_held, w_gate, w_up), refs = refs[:4], refs[4:]
    if last:
        w_down, hidden, down_next, x, gate_ring, up_ring, sems, next_sems, gate_sum, up_sum = refs
    else:
        gate_sum, up_sum, gate_next, up_next, x, gate_ring, up_ring, sems, next_sems = refs
    hid = w_gate.shape[1]
    width = x.shape[0] // len(parts)
    per = width // kb
    start = parts[0] * per
    weights = (w_gate, w_up)

    def fetch(step, slot):
        places = (gate_ring.at[slot], up_ring.at[slot])
        return moves(weights, start + step, per, places, (sems.at[0, slot], sems.at[1, slot]))

    ahead = []
    for k in range(more):
        if last:
            down_per = width // down_next.shape[-1]
            ahead += moves((w_down,), down_per + k, down_per, (down_next.at[k],), (next_sems.at[0, k],))
        else:
            places = (gate_next.at[k], up_next.at[k])
            at = (next_sems.at[0, k], next_sems.at[1, k])
            ahead += moves(weights, start + per + k, per, places, at)

    def begin():
        for j in range(len(parts)):
            rows = [sent[2 * j + at][:, :width].astype(F32) for at in range(2)]
            x[j * width : (j + 1) * width] = jnp.concatenate(rows, axis=0).T.astype(BF16)
        gate_sum[...] = earlier[0][...] if last else jnp.zeros_like(gate_sum)
        up_sum[...] = earlier[1][...] if last else jnp.zeros_like(up_sum)

    def right(step):
        return x[pl.ds(pl.multiple_of(step * kb, LANES), kb)]

    def from_held(step):
        gate_sum[...] += jnp.dot(gate_held[step], right(step), preferred_element_type=F32)
        up_sum[...] += jnp.dot(up_held[step], right(step), preferred_element_type=F32)

    def from_ring(step, slot, waits):
        waits[0].wait()
        gate_sum[...] += jnp.dot(gate_ring[slot], right(step), preferred_element_type=F32)
        waits[1].wait()
        up_sum[...] += jnp.dot(up_ring[slot], right(step), preferred_element_type=F32)

    stream(held, len(parts) * per, fetch, ahead, begin, from_held, from_ring)
    if last:
        unit = largest_step(hid, (384,))
        for first in range(0, hid, unit):
            units = pl.ds(first, unit)
            gate = gate_sum[units]
            value = gate / (1.0 + jnp.exp(-gate)) * up_sum[units]
            hidden[:, units] = value.T.astype(BF16)
    finish(ahead)


def down_kernel(start, count, held, experts, shares, hidden, own, other, *refs):
    down_held, refs = (refs[0], refs[1:]) if held else (None, refs)
    w_down, *outs, ring, sems = refs
    unused, half, width = outs[0].shape
    fb = ring.shape[-1]
    per = width // fb
    expert = lax.axis_index("expert") // shares
    packed = jnp.concatenate([own[:, width:], other[:, width:]], axis=0).astype(F32)
    lane = lax.broadcasted_iota(jnp.int32, packed.shape, 1)
    mine = (lax.rem(lane, experts) == expert) & (lane < 3 * experts)
    coef = jnp.sum(jnp.where(mine, packed, 0.0), axis=1, keepdims=True)

    def fetch(step, slot):
        return moves((w_down,), start + step, per, (ring.at[slot],), (sems.at[slot],))

    def put(step, block):
        value = jnp.dot(hidden[...], block, preferred_element_type=F32) * coef
        columns = pl.ds(pl.multiple_of(lax.rem(step, per) * fb, LANES), fb)
        for at, out in enumerate(outs):
            out[step // per, :, columns] = value[at * half : (at + 1) * half].astype(out.dtype)

    def from_held(step):
        put(step, down_held[step])

    def from_ring(step, slot, waits):
        waits[0].wait()
        put(step, ring[slot])

    stream(held, count, fetch, (), lambda: None, from_held, from_ring)


def body(tokens, expert_ids, route_weight, w_gate, w_up, w_down):
    n_expert = lax.axis_size("expert")
    n_blk = lax.axis_size("blk")
    rows, width = tokens.shape
    top = expert_ids.shape[1]
    hid = w_gate.shape[1]
    shares = FFW // (hid * n_blk)
    experts = n_expert // shares
    places = n_expert // PAIR
    half = places * rows
    tokens_all = PAIR * half
    room = -(-3 * experts // LANES) * LANES
    vmem, hbm = pltpu.VMEM, pl.ANY
    w_gate, w_up, w_down = in_hbm(w_gate, w_up, w_down)

    (packed,) = call(
        functools.partial(pack_kernel, experts),
        [jax.ShapeDtypeStruct((rows, width + room), BF16)],
        in_hbm(tokens, expert_ids.T, route_weight.T),
        (hbm,) * 3,
        [
            pltpu.VMEM((rows, width), BF16),
            pltpu.VMEM((top, rows), jnp.int32),
            pltpu.VMEM((top, rows), F32),
            pltpu.SemaphoreType.DMA((3,)),
        ],
        8,
        rows * room,
        4 * rows * width,
    )

    def along(k):
        return [(s, ((s // PAIR + k) % places) * PAIR + s % PAIR) for s in range(n_expert)]

    def across(k):
        return [(s, (s + k) % n_blk) for s in range(n_blk)]

    def across_other(k):
        return [
            (s * n_blk + b, (s ^ 1) * n_blk + (b + k) % n_blk)
            for s in range(n_expert)
            for b in range(n_blk)
        ]

    swap = [(s, s ^ 1) for s in range(n_expert)]

    kb = largest_step(width, (512, 384, 256, 128))
    per = width // kb
    steps = per * (n_blk - 1)
    first_held, second_held, third_held = min(3, per), min(2, steps), min(3, steps)

    def blocks(count):
        return pltpu.VMEM((count, hid, kb), BF16)

    held = call(
        functools.partial(head_kernel, first_held, per),
        [blocks(first_held)] * 2,
        (packed, w_gate, w_up),
        (hbm,) * 3,
        [pltpu.SemaphoreType.DMA((2, first_held))],
        4,
        0,
        4 * hid * kb * first_held,
    )
    pieces = [packed] + [lax.ppermute(packed, "expert", along(k)) for k in range(1, places)]
    pieces, held = lax.optimization_barrier((pieces, held))
    own = jnp.concatenate(pieces, axis=0)
    other = lax.ppermute(own, "expert", swap)
    bare = own[:, :width]
    sent = []
    for j in range(1, n_blk):
        sent.append(lax.ppermute(bare, "blk", across(-j)))
        sent.append(lax.ppermute(bare, ("expert", "blk"), across_other(-j)))

    sums = [jax.ShapeDtypeStruct((hid, tokens_all), F32)] * 2

    def up(parts, held, more, last, outs, operands):
        weights = (w_gate, w_up, w_down) if last else (w_gate, w_up)
        return call(
            functools.partial(up_kernel, kb, parts, held, more, last),
            outs,
            (*operands, *weights),
            (vmem,) * len(operands) + (hbm,) * len(weights),
            [
                pltpu.VMEM((width * len(parts), tokens_all), BF16),
                blocks(SLOTS),
                blocks(SLOTS),
                pltpu.SemaphoreType.DMA((2, SLOTS)),
                pltpu.SemaphoreType.DMA((2, more)),
            ]
            + [pltpu.VMEM(each.shape, F32) for each in sums if last],
            23 if last else 20,
            4 * tokens_all * hid * width * len(parts),
            4 * hid * width * len(parts),
        )

    *partial_sums, gate_held, up_held = up(
        (0,), first_held, second_held, False, sums + [blocks(second_held)] * 2, (own, other, *held)
    )
    hidden, down_held = up(
        tuple(range(1, n_blk)),
        second_held,
        third_held,
        True,
        [jax.ShapeDtypeStruct((tokens_all, hid), BF16), blocks(third_held)],
        (*sent, *partial_sums, gate_held, up_held),
    )

    def down(first, count, kinds, *down_held):
        held = third_held if down_held else 0
        return call(
            functools.partial(down_kernel, first, count, held, experts, shares),
            [jax.ShapeDtypeStruct((count // per, half, width), kind) for kind in kinds],
            (hidden, own, other, *down_held, w_down),
            (vmem,) * (3 + len(down_held)) + (hbm,),
            [blocks(SLOTS), pltpu.SemaphoreType.DMA((SLOTS,))],
            14,
            2 * tokens_all * hid * kb * count,
            2 * hid * kb * count,
        )

    away = down(per, steps, (BF16, BF16), down_held)
    total = []
    for j in range(1, n_blk):
        total.append(lax.ppermute(away[0][j - 1], "blk", across(j)))
        total.append(lax.ppermute(away[1][j - 1], ("expert", "blk"), across_other(j)))
    kept, given = down(0, per, (F32, BF16))
    total.append(lax.ppermute(given[0], "expert", swap))
    summed = kept[0]
    for term in total:
        summed = summed + term.astype(F32)
    mixed = summed[:rows]
    for k in range(1, places):
        piece = summed[k * rows : (k + 1) * rows].astype(BF16)
        mixed = mixed + lax.ppermute(piece, "expert", along(-k)).astype(F32)
    return mixed.astype(BF16)


def solution(mesh):
    placed = (
        P(("groups", "expert"), "blk"),
        P(("groups", "expert"), None),
        P(("groups", "expert"), None),
        P("expert", "blk", None),
        P("expert", "blk", None),
        P("expert", "blk", None),
    )
    return jax.shard_map(
        body, mesh=mesh, in_specs=placed, out_specs=P(("groups", "expert"), "blk"), check_vma=False
    )
```

```python
import functools

import jax
import jax.numpy as jnp
from jax import lax
from jax.experimental import pallas as pl
from jax.experimental.pallas import tpu as pltpu
from jax.sharding import PartitionSpec as P

FFW = 5376
PAIR = 2
LANES = 128
UP_SLOTS = 2
DOWN_SLOTS = 3
MIB = 1024 * 1024
F32 = jnp.float32
BF16 = jnp.bfloat16


def largest_step(total, choices):
    for step in choices:
        if total % step == 0:
            return step
    return total


def call(kernel, outs, operands, spaces, scratch, limit, flops, moved):
    return pl.pallas_call(
        kernel,
        out_shape=outs,
        in_specs=[pl.BlockSpec(memory_space=space) for space in spaces],
        out_specs=[pl.BlockSpec(memory_space=pltpu.VMEM) for unused in outs],
        scratch_shapes=scratch,
        compiler_params=pltpu.CompilerParams(vmem_limit_bytes=limit * MIB),
        cost_estimate=pl.CostEstimate(flops=flops, bytes_accessed=moved, transcendentals=0),
    )(*operands)


def in_hbm(*arrays):
    return [pltpu.with_memory_space_constraint(array, pltpu.HBM) for array in arrays]


def columns_of(step, per, block):
    owner = lax.rem(lax.axis_index("blk") + step // per, lax.axis_size("blk"))
    return pl.ds(pl.multiple_of((owner * per + lax.rem(step, per)) * block, LANES), block)


def moves(weights, step, per, targets, sems):
    return [
        pltpu.make_async_copy(weight.at[0, :, columns_of(step, per, target.shape[-1])], target, sem)
        for weight, target, sem in zip(weights, targets, sems)
    ]


def stream(held, count, slots, fetch, ahead, begin, from_held, from_ring):
    rest = count - held
    for at in range(min(slots, rest)):
        for copy in fetch(held + at, at):
            copy.start()
    if rest == 0:
        for copy in ahead:
            copy.start()
    begin()

    def first(step, carry):
        from_held(step)
        return carry

    if held:
        lax.fori_loop(0, held, first, 0)

    def then(at, carry):
        later = at + slots - 1

        @pl.when((at > 0) & (later < rest))
        def _():
            for copy in fetch(held + later, lax.rem(later, slots)):
                copy.start()

        @pl.when(at == max(rest - slots, 0))
        def _():
            for copy in ahead:
                copy.start()

        slot = lax.rem(at, slots)
        from_ring(held + at, slot, fetch(held + at, slot))
        return carry

    if rest:
        lax.fori_loop(0, rest, then, 0)


def finish(copies):
    for copy in copies:
        copy.wait()


def head_kernel(count, per, after, w_gate, w_up, gate, up, sems):
    copies = []
    for step in range(count):
        at = (sems.at[0, step], sems.at[1, step])
        copies += moves((w_gate, w_up), step, per, (gate.at[step], up.at[step]), at)
    for copy in copies:
        copy.start()
    finish(copies)


def pack_kernel(experts, tokens, ids, weights, out, held, named, weighed, sems):
    copies = [
        pltpu.make_async_copy(source, target, sems.at[at])
        for at, (source, target) in enumerate(((ids, named), (weights, weighed), (tokens, held)))
    ]
    for copy in copies:
        copy.start()
    rows, width = tokens.shape
    shape = (rows, out.shape[1] - width)
    lane = lax.broadcasted_iota(jnp.int32, shape, 1)
    diagonal = lax.broadcasted_iota(jnp.int32, (rows, rows), 0) == lax.broadcasted_iota(
        jnp.int32, (rows, rows), 1
    )
    coef = jnp.zeros(shape, F32)
    copies[0].wait()
    copies[1].wait()
    for k in range(ids.shape[0]):
        name = jnp.sum(jnp.where(diagonal, named[k : k + 1], 0), axis=1, keepdims=True)
        weight = jnp.sum(jnp.where(diagonal, weighed[k : k + 1], 0.0), axis=1, keepdims=True)
        coef += jnp.where(lax.rem(lane, experts) == name, weight, 0.0)
    high = coef.astype(BF16).astype(F32)
    middle = (coef - high).astype(BF16).astype(F32)
    low = coef - high - middle
    part = jnp.where(lane < experts, high, jnp.where(lane < 2 * experts, middle, low))
    out[:, width:] = jnp.where(lane < 3 * experts, part, 0.0).astype(BF16)
    copies[2].wait()
    out[:, :width] = held[...]


def up_kernel(kb, parts, held, more, last, *refs):
    sent, refs = refs[: 2 * len(parts)], refs[2 * len(parts) :]
    earlier, refs = (refs[:2], refs[2:]) if last else ((), refs)
    (gate_held, up_held, w_gate, w_up), refs = refs[:4], refs[4:]
    if last:
        w_down, hidden, down_next, x, gate_ring, up_ring, sems, next_sems, gate_sum, up_sum = refs
    else:
        gate_sum, up_sum, gate_next, up_next, x, gate_ring, up_ring, sems, next_sems = refs
    hid = w_gate.shape[1]
    width = x.shape[0] // len(parts)
    per = width // kb
    start = parts[0] * per
    weights = (w_gate, w_up)

    def fetch(step, slot):
        places = (gate_ring.at[slot], up_ring.at[slot])
        return moves(weights, start + step, per, places, (sems.at[0, slot], sems.at[1, slot]))

    ahead = []
    for k in range(more):
        if last:
            down_per = width // down_next.shape[-1]
            ahead += moves((w_down,), down_per + k, down_per, (down_next.at[k],), (next_sems.at[0, k],))
        else:
            places = (gate_next.at[k], up_next.at[k])
            at = (next_sems.at[0, k], next_sems.at[1, k])
            ahead += moves(weights, start + per + k, per, places, at)

    def begin():
        for j in range(len(parts)):
            rows = [sent[2 * j + at][:, :width].astype(F32) for at in range(2)]
            x[j * width : (j + 1) * width] = jnp.concatenate(rows, axis=0).T.astype(BF16)
        gate_sum[...] = earlier[0][...] if last else jnp.zeros_like(gate_sum)
        up_sum[...] = earlier[1][...] if last else jnp.zeros_like(up_sum)

    def right(step):
        return x[pl.ds(pl.multiple_of(step * kb, LANES), kb)]

    def from_held(step):
        gate_sum[...] += jnp.dot(gate_held[step], right(step), preferred_element_type=F32)
        up_sum[...] += jnp.dot(up_held[step], right(step), preferred_element_type=F32)

    def from_ring(step, slot, waits):
        waits[0].wait()
        gate_sum[...] += jnp.dot(gate_ring[slot], right(step), preferred_element_type=F32)
        waits[1].wait()
        up_sum[...] += jnp.dot(up_ring[slot], right(step), preferred_element_type=F32)

    stream(held, len(parts) * per, gate_ring.shape[0], fetch, ahead, begin, from_held, from_ring)
    if last:
        unit = largest_step(hid, (384,))
        for first in range(0, hid, unit):
            units = pl.ds(first, unit)
            gate = gate_sum[units]
            value = gate / (1.0 + jnp.exp(-gate)) * up_sum[units]
            hidden[:, units] = value.T.astype(BF16)
    finish(ahead)


def down_kernel(start, count, held, experts, shares, hidden, own, other, *refs):
    down_held, refs = (refs[0], refs[1:]) if held else (None, refs)
    w_down, *outs, ring, sems = refs
    unused, half, width = outs[0].shape
    fb = ring.shape[-1]
    per = width // fb
    expert = lax.axis_index("expert") // shares
    packed = jnp.concatenate([own[:, width:], other[:, width:]], axis=0).astype(F32)
    lane = lax.broadcasted_iota(jnp.int32, packed.shape, 1)
    mine = (lax.rem(lane, experts) == expert) & (lane < 3 * experts)
    coef = jnp.sum(jnp.where(mine, packed, 0.0), axis=1, keepdims=True)

    def fetch(step, slot):
        return moves((w_down,), start + step, per, (ring.at[slot],), (sems.at[slot],))

    def put(step, block):
        value = jnp.dot(hidden[...], block, preferred_element_type=F32) * coef
        columns = pl.ds(pl.multiple_of(lax.rem(step, per) * fb, LANES), fb)
        for at, out in enumerate(outs):
            out[step // per, :, columns] = value[at * half : (at + 1) * half].astype(out.dtype)

    def from_held(step):
        put(step, down_held[step])

    def from_ring(step, slot, waits):
        waits[0].wait()
        put(step, ring[slot])

    stream(held, count, ring.shape[0], fetch, (), lambda: None, from_held, from_ring)


def body(tokens, expert_ids, route_weight, w_gate, w_up, w_down):
    n_expert = lax.axis_size("expert")
    n_blk = lax.axis_size("blk")
    rows, width = tokens.shape
    top = expert_ids.shape[1]
    hid = w_gate.shape[1]
    shares = FFW // (hid * n_blk)
    experts = n_expert // shares
    places = n_expert // PAIR
    half = places * rows
    tokens_all = PAIR * half
    room = -(-3 * experts // LANES) * LANES
    vmem, hbm = pltpu.VMEM, pl.ANY
    w_gate, w_up, w_down = in_hbm(w_gate, w_up, w_down)

    (packed,) = call(
        functools.partial(pack_kernel, experts),
        [jax.ShapeDtypeStruct((rows, width + room), BF16)],
        in_hbm(tokens, expert_ids.T, route_weight.T),
        (hbm,) * 3,
        [
            pltpu.VMEM((rows, width), BF16),
            pltpu.VMEM((top, rows), jnp.int32),
            pltpu.VMEM((top, rows), F32),
            pltpu.SemaphoreType.DMA((3,)),
        ],
        8,
        rows * room,
        4 * rows * width,
    )

    def along(k):
        return [(s, (s // PAIR ^ k) * PAIR + s % PAIR) for s in range(n_expert)]

    def across(k):
        return [(s, (s + k) % n_blk) for s in range(n_blk)]

    def across_other(k):
        return [
            (s * n_blk + b, (s ^ 1) * n_blk + (b + k) % n_blk)
            for s in range(n_expert)
            for b in range(n_blk)
        ]

    swap = [(s, s ^ 1) for s in range(n_expert)]

    kb = largest_step(width, (1024, 768, 512, 384, 256, 128))
    fb = largest_step(width, (512, 384, 256, 128))
    per, down_per = width // kb, width // fb
    up_held, down_held = 1, min(3, down_per)

    def blocks(count, block):
        return pltpu.VMEM((count, hid, block), BF16)

    held = call(
        functools.partial(head_kernel, up_held, per),
        [blocks(up_held, kb)] * 2,
        (packed, w_gate, w_up),
        (hbm,) * 3,
        [pltpu.SemaphoreType.DMA((2, up_held))],
        4,
        0,
        4 * hid * kb * up_held,
    )
    pieces = [packed] + [lax.ppermute(packed, "expert", along(k)) for k in range(1, places)]
    pieces, held = lax.optimization_barrier((pieces, held))
    own = jnp.concatenate(pieces, axis=0)
    other = lax.ppermute(own, "expert", swap)
    bare = own[:, :width]
    sent = []
    for j in range(1, n_blk):
        sent.append(lax.ppermute(bare, "blk", across(-j)))
        sent.append(lax.ppermute(bare, ("expert", "blk"), across_other(-j)))

    sums = [jax.ShapeDtypeStruct((hid, tokens_all), F32)] * 2

    def up(parts, more, outs, operands):
        last = parts[0] > 0
        weights = (w_gate, w_up, w_down) if last else (w_gate, w_up)
        return call(
            functools.partial(up_kernel, kb, parts, up_held, more, last),
            outs,
            (*operands, *weights),
            (vmem,) * len(operands) + (hbm,) * len(weights),
            [
                pltpu.VMEM((width * len(parts), tokens_all), BF16),
                blocks(UP_SLOTS, kb),
                blocks(UP_SLOTS, kb),
                pltpu.SemaphoreType.DMA((2, UP_SLOTS)),
                pltpu.SemaphoreType.DMA((2, more)),
            ]
            + [pltpu.VMEM(each.shape, F32) for each in sums if last],
            35 if last else 33,
            4 * tokens_all * hid * width * len(parts),
            4 * hid * width * len(parts),
        )

    begun = up((0,), up_held, sums + [blocks(up_held, kb)] * 2, (own, other, *held))
    hidden, first_blocks = up(
        tuple(range(1, n_blk)),
        down_held,
        [jax.ShapeDtypeStruct((tokens_all, hid), BF16), blocks(down_held, fb)],
        (*sent, *begun),
    )

    def down(first, count, kinds, *held):
        return call(
            functools.partial(down_kernel, first, count, down_held * len(held), experts, shares),
            [jax.ShapeDtypeStruct((count // down_per, half, width), kind) for kind in kinds],
            (hidden, own, other, *held, w_down),
            (vmem,) * (3 + len(held)) + (hbm,),
            [blocks(DOWN_SLOTS, fb), pltpu.SemaphoreType.DMA((DOWN_SLOTS,))],
            20,
            2 * tokens_all * hid * fb * count,
            2 * hid * fb * count,
        )

    away = down(down_per, down_per * (n_blk - 1), (BF16, BF16), first_blocks)
    total = []
    for j in range(1, n_blk):
        total.append(lax.ppermute(away[0][j - 1], "blk", across(j)))
        total.append(lax.ppermute(away[1][j - 1], ("expert", "blk"), across_other(j)))
    kept, given = down(0, down_per, (F32, BF16))
    total.append(lax.ppermute(given[0], "expert", swap))
    summed = kept[0]
    for term in total:
        summed = summed + term.astype(F32)
    pieces = {k: summed[k * rows : (k + 1) * rows] for k in range(places)}
    bit = 1
    while bit < places:
        leaving = [k for k in pieces if k & bit]
        piece = jnp.concatenate([pieces[k] for k in leaving], axis=0).astype(BF16)
        piece = lax.ppermute(piece, "expert", along(bit)).astype(F32)
        pieces = {k ^ bit: pieces[k ^ bit] + piece[at * rows : (at + 1) * rows] for at, k in enumerate(leaving)}
        bit *= 2
    return pieces[0].astype(BF16)


def solution(mesh):
    placed = (
        P(("groups", "expert"), "blk"),
        P(("groups", "expert"), None),
        P(("groups", "expert"), None),
        P("expert", "blk", None),
        P("expert", "blk", None),
        P("expert", "blk", None),
    )
    return jax.shard_map(
        body, mesh=mesh, in_specs=placed, out_specs=P(("groups", "expert"), "blk"), check_vma=False
    )
```

```python
import functools

import jax
import jax.numpy as jnp
from jax import lax
from jax.experimental import pallas as pl
from jax.experimental.pallas import tpu as pltpu
from jax.sharding import PartitionSpec as P

FFW = 5376
PAIR = 2
LANES = 128
SLOTS = 3
MIB = 1024 * 1024
F32 = jnp.float32
BF16 = jnp.bfloat16


def largest_step(total, choices):
    for step in choices:
        if total % step == 0:
            return step
    return total


def call(kernel, outs, operands, spaces, scratch, limit, flops, moved):
    return pl.pallas_call(
        kernel,
        out_shape=outs,
        in_specs=[pl.BlockSpec(memory_space=space) for space in spaces],
        out_specs=[pl.BlockSpec(memory_space=pltpu.VMEM) for unused in outs],
        scratch_shapes=scratch,
        compiler_params=pltpu.CompilerParams(vmem_limit_bytes=limit * MIB),
        cost_estimate=pl.CostEstimate(flops=flops, bytes_accessed=moved, transcendentals=0),
    )(*operands)


def in_hbm(*arrays):
    return [pltpu.with_memory_space_constraint(array, pltpu.HBM) for array in arrays]


def columns_of(step, per, block):
    owner = lax.rem(lax.axis_index("blk") + step // per, lax.axis_size("blk"))
    return pl.ds(pl.multiple_of((owner * per + lax.rem(step, per)) * block, LANES), block)


def moves(weights, step, per, targets, sems):
    return [
        pltpu.make_async_copy(weight.at[0, :, columns_of(step, per, target.shape[-1])], target, sem)
        for weight, target, sem in zip(weights, targets, sems)
    ]


def stream(held, count, fetch, ahead, begin, from_held, from_ring):
    rest = count - held
    for at in range(min(SLOTS, rest)):
        for copy in fetch(held + at, at):
            copy.start()
    if rest == 0:
        for copy in ahead:
            copy.start()
    begin()

    def first(step, carry):
        from_held(step)
        return carry

    if held:
        lax.fori_loop(0, held, first, 0)

    def then(at, carry):
        later = at + SLOTS - 1

        @pl.when((at > 0) & (later < rest))
        def _():
            for copy in fetch(held + later, lax.rem(later, SLOTS)):
                copy.start()

        @pl.when(at == max(rest - SLOTS, 0))
        def _():
            for copy in ahead:
                copy.start()

        slot = lax.rem(at, SLOTS)
        from_ring(held + at, slot, fetch(held + at, slot))
        return carry

    if rest:
        lax.fori_loop(0, rest, then, 0)


def finish(copies):
    for copy in copies:
        copy.wait()


def head_kernel(count, per, after, w_gate, w_up, gate, up, sems):
    copies = []
    for step in range(count):
        at = (sems.at[0, step], sems.at[1, step])
        copies += moves((w_gate, w_up), step, per, (gate.at[step], up.at[step]), at)
    for copy in copies:
        copy.start()
    finish(copies)


def pack_kernel(experts, tokens, ids, weights, out, held, named, weighed, sems):
    copies = [
        pltpu.make_async_copy(source, target, sems.at[at])
        for at, (source, target) in enumerate(((ids, named), (weights, weighed), (tokens, held)))
    ]
    for copy in copies:
        copy.start()
    rows, width = tokens.shape
    shape = (rows, out.shape[1] - width)
    lane = lax.broadcasted_iota(jnp.int32, shape, 1)
    diagonal = lax.broadcasted_iota(jnp.int32, (rows, rows), 0) == lax.broadcasted_iota(
        jnp.int32, (rows, rows), 1
    )
    coef = jnp.zeros(shape, F32)
    copies[0].wait()
    copies[1].wait()
    for k in range(ids.shape[0]):
        name = jnp.sum(jnp.where(diagonal, named[k : k + 1], 0), axis=1, keepdims=True)
        weight = jnp.sum(jnp.where(diagonal, weighed[k : k + 1], 0.0), axis=1, keepdims=True)
        coef += jnp.where(lax.rem(lane, experts) == name, weight, 0.0)
    high = coef.astype(BF16).astype(F32)
    middle = (coef - high).astype(BF16).astype(F32)
    low = coef - high - middle
    part = jnp.where(lane < experts, high, jnp.where(lane < 2 * experts, middle, low))
    out[:, width:] = jnp.where(lane < 3 * experts, part, 0.0).astype(BF16)
    copies[2].wait()
    out[:, :width] = held[...]


def up_kernel(kb, parts, held, more, last, *refs):
    sent, refs = refs[: 2 * len(parts)], refs[2 * len(parts) :]
    earlier, refs = (refs[:2], refs[2:]) if last else ((), refs)
    (gate_held, up_held, w_gate, w_up), refs = refs[:4], refs[4:]
    if last:
        w_down, hidden, down_next, x, gate_ring, up_ring, sems, next_sems, gate_sum, up_sum = refs
    else:
        gate_sum, up_sum, gate_next, up_next, x, gate_ring, up_ring, sems, next_sems = refs
    hid = w_gate.shape[1]
    width = x.shape[0] // len(parts)
    per = width // kb
    start = parts[0] * per
    weights = (w_gate, w_up)

    def fetch(step, slot):
        places = (gate_ring.at[slot], up_ring.at[slot])
        return moves(weights, start + step, per, places, (sems.at[0, slot], sems.at[1, slot]))

    ahead = []
    for k in range(more):
        if last:
            down_per = width // down_next.shape[-1]
            ahead += moves((w_down,), down_per + k, down_per, (down_next.at[k],), (next_sems.at[0, k],))
        else:
            places = (gate_next.at[k], up_next.at[k])
            at = (next_sems.at[0, k], next_sems.at[1, k])
            ahead += moves(weights, start + per + k, per, places, at)

    def begin():
        for j in range(len(parts)):
            rows = [sent[2 * j + at][:, :width].astype(F32) for at in range(2)]
            x[j * width : (j + 1) * width] = jnp.concatenate(rows, axis=0).T.astype(BF16)
        gate_sum[...] = earlier[0][...] if last else jnp.zeros_like(gate_sum)
        up_sum[...] = earlier[1][...] if last else jnp.zeros_like(up_sum)

    part = largest_step(hid, (448, 384, 256, 128))
    several = 3 if hid % (3 * part) == 0 else 1

    def add(total, block, step):
        right = x[pl.ds(pl.multiple_of(step * kb, LANES), kb)]

        def some(at, carry):
            for k in range(several):
                rows = pl.ds(pl.multiple_of((at * several + k) * part, 16), part)
                total[rows] += jnp.dot(block[rows], right, preferred_element_type=F32)
            return carry

        lax.fori_loop(0, hid // (several * part), some, 0)

    def from_held(step):
        add(gate_sum, gate_held.at[step], step)
        add(up_sum, up_held.at[step], step)

    def from_ring(step, slot, waits):
        waits[0].wait()
        add(gate_sum, gate_ring.at[slot], step)
        waits[1].wait()
        add(up_sum, up_ring.at[slot], step)

    stream(held, len(parts) * per, fetch, ahead, begin, from_held, from_ring)
    if last:
        unit = largest_step(hid, (384,))
        for first in range(0, hid, unit):
            units = pl.ds(first, unit)
            gate = gate_sum[units]
            value = gate / (1.0 + jnp.exp(-gate)) * up_sum[units]
            hidden[:, units] = value.T.astype(BF16)
    finish(ahead)


def down_kernel(start, count, held, experts, shares, hidden, own, other, *refs):
    down_held, refs = (refs[0], refs[1:]) if held else (None, refs)
    w_down, *outs, ring, sems = refs
    unused, half, width = outs[0].shape
    fb = ring.shape[-1]
    per = width // fb
    expert = lax.axis_index("expert") // shares
    packed = jnp.concatenate([own[:, width:], other[:, width:]], axis=0).astype(F32)
    lane = lax.broadcasted_iota(jnp.int32, packed.shape, 1)
    mine = (lax.rem(lane, experts) == expert) & (lane < 3 * experts)
    coef = jnp.sum(jnp.where(mine, packed, 0.0), axis=1, keepdims=True)

    def fetch(step, slot):
        return moves((w_down,), start + step, per, (ring.at[slot],), (sems.at[slot],))

    def put(step, block):
        value = jnp.dot(hidden[...], block, preferred_element_type=F32) * coef
        columns = pl.ds(pl.multiple_of(lax.rem(step, per) * fb, LANES), fb)
        for at, out in enumerate(outs):
            out[step // per, :, columns] = value[at * half : (at + 1) * half].astype(out.dtype)

    def from_held(step):
        put(step, down_held[step])

    def from_ring(step, slot, waits):
        waits[0].wait()
        put(step, ring[slot])

    stream(held, count, fetch, (), lambda: None, from_held, from_ring)


def body(tokens, expert_ids, route_weight, w_gate, w_up, w_down):
    n_expert = lax.axis_size("expert")
    n_blk = lax.axis_size("blk")
    rows, width = tokens.shape
    top = expert_ids.shape[1]
    hid = w_gate.shape[1]
    shares = FFW // (hid * n_blk)
    experts = n_expert // shares
    places = n_expert // PAIR
    half = places * rows
    tokens_all = PAIR * half
    room = -(-3 * experts // LANES) * LANES
    vmem, hbm = pltpu.VMEM, pl.ANY
    w_gate, w_up, w_down = in_hbm(w_gate, w_up, w_down)

    (packed,) = call(
        functools.partial(pack_kernel, experts),
        [jax.ShapeDtypeStruct((rows, width + room), BF16)],
        in_hbm(tokens, expert_ids.T, route_weight.T),
        (hbm,) * 3,
        [
            pltpu.VMEM((rows, width), BF16),
            pltpu.VMEM((top, rows), jnp.int32),
            pltpu.VMEM((top, rows), F32),
            pltpu.SemaphoreType.DMA((3,)),
        ],
        8,
        rows * room,
        4 * rows * width,
    )

    def along(k):
        return [(s, ((s // PAIR + k) % places) * PAIR + s % PAIR) for s in range(n_expert)]

    def across(k):
        return [(s, (s + k) % n_blk) for s in range(n_blk)]

    def across_other(k):
        return [
            (s * n_blk + b, (s ^ 1) * n_blk + (b + k) % n_blk)
            for s in range(n_expert)
            for b in range(n_blk)
        ]

    swap = [(s, s ^ 1) for s in range(n_expert)]

    kb = largest_step(width, (512, 384, 256, 128))
    per = width // kb
    steps = per * (n_blk - 1)
    first_held, second_held, third_held = min(2, per), min(1, steps), min(3, steps)

    def blocks(count):
        return pltpu.VMEM((count, hid, kb), BF16)

    held = call(
        functools.partial(head_kernel, first_held, per),
        [blocks(first_held)] * 2,
        (packed, w_gate, w_up),
        (hbm,) * 3,
        [pltpu.SemaphoreType.DMA((2, first_held))],
        4,
        0,
        4 * hid * kb * first_held,
    )
    pieces = [packed] + [lax.ppermute(packed, "expert", along(k)) for k in range(1, places)]
    pieces, held = lax.optimization_barrier((pieces, held))
    own = jnp.concatenate(pieces, axis=0)
    other = lax.ppermute(own, "expert", swap)
    bare = own[:, :width]
    sent = []
    for j in range(1, n_blk):
        sent.append(lax.ppermute(bare, "blk", across(-j)))
        sent.append(lax.ppermute(bare, ("expert", "blk"), across_other(-j)))

    sums = [jax.ShapeDtypeStruct((hid, tokens_all), F32)] * 2

    def up(parts, held, more, last, outs, operands):
        weights = (w_gate, w_up, w_down) if last else (w_gate, w_up)
        return call(
            functools.partial(up_kernel, kb, parts, held, more, last),
            outs,
            (*operands, *weights),
            (vmem,) * len(operands) + (hbm,) * len(weights),
            [
                pltpu.VMEM((width * len(parts), tokens_all), BF16),
                blocks(SLOTS),
                blocks(SLOTS),
                pltpu.SemaphoreType.DMA((2, SLOTS)),
                pltpu.SemaphoreType.DMA((2, more)),
            ]
            + [pltpu.VMEM(each.shape, F32) for each in sums if last],
            23 if last else 20,
            4 * tokens_all * hid * width * len(parts),
            4 * hid * width * len(parts),
        )

    *partial_sums, gate_held, up_held = up(
        (0,), first_held, second_held, False, sums + [blocks(second_held)] * 2, (own, other, *held)
    )
    hidden, down_held = up(
        tuple(range(1, n_blk)),
        second_held,
        third_held,
        True,
        [jax.ShapeDtypeStruct((tokens_all, hid), BF16), blocks(third_held)],
        (*sent, *partial_sums, gate_held, up_held),
    )

    def down(first, count, kinds, *down_held):
        held = third_held if down_held else 0
        return call(
            functools.partial(down_kernel, first, count, held, experts, shares),
            [jax.ShapeDtypeStruct((count // per, half, width), kind) for kind in kinds],
            (hidden, own, other, *down_held, w_down),
            (vmem,) * (3 + len(down_held)) + (hbm,),
            [blocks(SLOTS), pltpu.SemaphoreType.DMA((SLOTS,))],
            14,
            2 * tokens_all * hid * kb * count,
            2 * hid * kb * count,
        )

    away = down(per, steps, (BF16, BF16), down_held)
    total = []
    for j in range(1, n_blk):
        total.append(lax.ppermute(away[0][j - 1], "blk", across(j)))
        total.append(lax.ppermute(away[1][j - 1], ("expert", "blk"), across_other(j)))
    kept, given = down(0, per, (F32, BF16))
    total.append(lax.ppermute(given[0], "expert", swap))
    summed = kept[0]
    for term in total:
        summed = summed + term.astype(F32)
    mixed = summed[:rows]
    for k in range(1, places):
        piece = summed[k * rows : (k + 1) * rows].astype(BF16)
        mixed = mixed + lax.ppermute(piece, "expert", along(-k)).astype(F32)
    return mixed.astype(BF16)


def solution(mesh):
    placed = (
        P(("groups", "expert"), "blk"),
        P(("groups", "expert"), None),
        P(("groups", "expert"), None),
        P("expert", "blk", None),
        P("expert", "blk", None),
        P("expert", "blk", None),
    )
    return jax.shard_map(
        body, mesh=mesh, in_specs=placed, out_specs=P(("groups", "expert"), "blk"), check_vma=False
    )
```

```python
import functools

import jax
import jax.numpy as jnp
from jax import lax
from jax.experimental import pallas as pl
from jax.experimental.pallas import tpu as pltpu
from jax.sharding import PartitionSpec as P

FFW = 5376
PAIR = 2
LANES = 128
SLOTS = 3
MIB = 1024 * 1024
F32 = jnp.float32
BF16 = jnp.bfloat16


def largest_step(total, choices):
    for step in choices:
        if total % step == 0:
            return step
    return total


def call(kernel, outs, operands, spaces, scratch, limit, flops, moved):
    return pl.pallas_call(
        kernel,
        out_shape=outs,
        in_specs=[pl.BlockSpec(memory_space=space) for space in spaces],
        out_specs=[pl.BlockSpec(memory_space=pltpu.VMEM) for unused in outs],
        scratch_shapes=scratch,
        compiler_params=pltpu.CompilerParams(vmem_limit_bytes=limit * MIB),
        cost_estimate=pl.CostEstimate(flops=flops, bytes_accessed=moved, transcendentals=0),
    )(*operands)


def in_hbm(*arrays):
    return [pltpu.with_memory_space_constraint(array, pltpu.HBM) for array in arrays]


def columns_of(step, per, block):
    owner = lax.rem(lax.axis_index("blk") + step // per, lax.axis_size("blk"))
    return pl.ds(pl.multiple_of((owner * per + lax.rem(step, per)) * block, LANES), block)


def moves(weights, step, per, targets, sems):
    return [
        pltpu.make_async_copy(weight.at[0, :, columns_of(step, per, target.shape[-1])], target, sem)
        for weight, target, sem in zip(weights, targets, sems)
    ]


def stream(held, count, fetch, ahead, begin, from_held, from_ring):
    rest = count - held
    for at in range(min(SLOTS, rest)):
        for copy in fetch(held + at, at):
            copy.start()
    if rest == 0:
        for copy in ahead:
            copy.start()
    begin()

    def first(step, carry):
        from_held(step)
        return carry

    if held:
        lax.fori_loop(0, held, first, 0)

    def then(at, carry):
        later = at + SLOTS - 1

        @pl.when((at > 0) & (later < rest))
        def _():
            for copy in fetch(held + later, lax.rem(later, SLOTS)):
                copy.start()

        @pl.when(at == max(rest - SLOTS, 0))
        def _():
            for copy in ahead:
                copy.start()

        slot = lax.rem(at, SLOTS)
        from_ring(held + at, slot, fetch(held + at, slot))
        return carry

    if rest:
        lax.fori_loop(0, rest, then, 0)


def finish(copies):
    for copy in copies:
        copy.wait()


def head_kernel(count, per, after, w_gate, w_up, gate, up, sems):
    copies = []
    for step in range(count):
        at = (sems.at[0, step], sems.at[1, step])
        copies += moves((w_gate, w_up), step, per, (gate.at[step], up.at[step]), at)
    for copy in copies:
        copy.start()
    finish(copies)


def pack_kernel(experts, tokens, ids, weights, out, held, named, weighed, sems):
    copies = [
        pltpu.make_async_copy(source, target, sems.at[at])
        for at, (source, target) in enumerate(((ids, named), (weights, weighed), (tokens, held)))
    ]
    for copy in copies:
        copy.start()
    rows, width = tokens.shape
    shape = (rows, out.shape[1] - width)
    lane = lax.broadcasted_iota(jnp.int32, shape, 1)
    diagonal = lax.broadcasted_iota(jnp.int32, (rows, rows), 0) == lax.broadcasted_iota(
        jnp.int32, (rows, rows), 1
    )
    coef = jnp.zeros(shape, F32)
    copies[0].wait()
    copies[1].wait()
    for k in range(ids.shape[0]):
        name = jnp.sum(jnp.where(diagonal, named[k : k + 1], 0), axis=1, keepdims=True)
        weight = jnp.sum(jnp.where(diagonal, weighed[k : k + 1], 0.0), axis=1, keepdims=True)
        coef += jnp.where(lax.rem(lane, experts) == name, weight, 0.0)
    high = coef.astype(BF16).astype(F32)
    middle = (coef - high).astype(BF16).astype(F32)
    low = coef - high - middle
    part = jnp.where(lane < experts, high, jnp.where(lane < 2 * experts, middle, low))
    out[:, width:] = jnp.where(lane < 3 * experts, part, 0.0).astype(BF16)
    copies[2].wait()
    out[:, :width] = held[...]


def up_kernel(kb, parts, held, more, last, *refs):
    sent, refs = refs[: 2 * len(parts)], refs[2 * len(parts) :]
    earlier, refs = (refs[:2], refs[2:]) if last else ((), refs)
    (gate_held, up_held, w_gate, w_up), refs = refs[:4], refs[4:]
    if last:
        w_down, hidden, down_next, x, gate_ring, up_ring, sems, next_sems, gate_sum, up_sum = refs
    else:
        gate_sum, up_sum, gate_next, up_next, x, gate_ring, up_ring, sems, next_sems = refs
    hid = w_gate.shape[1]
    width = x.shape[0] // len(parts)
    per = width // kb
    start = parts[0] * per
    weights = (w_gate, w_up)

    def fetch(step, slot):
        places = (gate_ring.at[slot], up_ring.at[slot])
        return moves(weights, start + step, per, places, (sems.at[0, slot], sems.at[1, slot]))

    ahead = []
    for k in range(more):
        if last:
            down_per = width // down_next.shape[-1]
            ahead += moves((w_down,), down_per + k, down_per, (down_next.at[k],), (next_sems.at[0, k],))
        else:
            places = (gate_next.at[k], up_next.at[k])
            at = (next_sems.at[0, k], next_sems.at[1, k])
            ahead += moves(weights, start + per + k, per, places, at)

    def begin():
        for j in range(len(parts)):
            rows = [sent[2 * j + at][:, :width].astype(F32) for at in range(2)]
            x[j * width : (j + 1) * width] = jnp.concatenate(rows, axis=0).T.astype(BF16)
        gate_sum[...] = earlier[0][...] if last else jnp.zeros_like(gate_sum)
        up_sum[...] = earlier[1][...] if last else jnp.zeros_like(up_sum)

    def right(step):
        return x[pl.ds(pl.multiple_of(step * kb, LANES), kb)]

    def from_held(step):
        gate_sum[...] += jnp.dot(gate_held[step], right(step), preferred_element_type=F32)
        up_sum[...] += jnp.dot(up_held[step], right(step), preferred_element_type=F32)

    def from_ring(step, slot, waits):
        waits[0].wait()
        gate_sum[...] += jnp.dot(gate_ring[slot], right(step), preferred_element_type=F32)
        waits[1].wait()
        up_sum[...] += jnp.dot(up_ring[slot], right(step), preferred_element_type=F32)

    stream(held, len(parts) * per, fetch, ahead, begin, from_held, from_ring)
    if last:
        unit = largest_step(hid, (384,))
        for first in range(0, hid, unit):
            units = pl.ds(first, unit)
            gate = gate_sum[units]
            value = gate / (1.0 + jnp.exp(-gate)) * up_sum[units]
            hidden[:, units] = value.T.astype(BF16)
    finish(ahead)


def down_kernel(width, start, count, held, more, experts, shares, hidden, own, other, *refs):
    down_held, refs = (refs[0], refs[1:]) if held else (None, refs)
    w_down, *outs, ring, sems, next_sems = refs
    down_next = outs.pop() if more else None
    unused, half, span = outs[0].shape
    fb = ring.shape[-1]
    per, inside = width // fb, span // fb
    expert = lax.axis_index("expert") // shares
    packed = jnp.concatenate([own[:, width:], other[:, width:]], axis=0).astype(F32)
    lane = lax.broadcasted_iota(jnp.int32, packed.shape, 1)
    mine = (lax.rem(lane, experts) == expert) & (lane < 3 * experts)
    coef = jnp.sum(jnp.where(mine, packed, 0.0), axis=1, keepdims=True)

    def fetch(step, slot):
        return moves((w_down,), start + step, per, (ring.at[slot],), (sems.at[slot],))

    def put(step, block):
        value = jnp.dot(hidden[...], block, preferred_element_type=F32) * coef
        columns = pl.ds(pl.multiple_of(lax.rem(step, inside) * fb, LANES), fb)
        for at, out in enumerate(outs):
            out[step // inside, :, columns] = value[at * half : (at + 1) * half].astype(out.dtype)

    def from_held(step):
        put(step, down_held[step])

    def from_ring(step, slot, waits):
        waits[0].wait()
        put(step, ring[slot])

    ahead = []
    for k in range(more):
        ahead += moves((w_down,), k, per, (down_next.at[k],), (next_sems.at[k],))
    stream(held, count, fetch, ahead, lambda: None, from_held, from_ring)
    finish(ahead)


def body(tokens, expert_ids, route_weight, w_gate, w_up, w_down):
    n_expert = lax.axis_size("expert")
    n_blk = lax.axis_size("blk")
    rows, width = tokens.shape
    top = expert_ids.shape[1]
    hid = w_gate.shape[1]
    shares = FFW // (hid * n_blk)
    experts = n_expert // shares
    places = n_expert // PAIR
    half = places * rows
    tokens_all = PAIR * half
    room = -(-3 * experts // LANES) * LANES
    vmem, hbm = pltpu.VMEM, pl.ANY
    w_gate, w_up, w_down = in_hbm(w_gate, w_up, w_down)

    (packed,) = call(
        functools.partial(pack_kernel, experts),
        [jax.ShapeDtypeStruct((rows, width + room), BF16)],
        in_hbm(tokens, expert_ids.T, route_weight.T),
        (hbm,) * 3,
        [
            pltpu.VMEM((rows, width), BF16),
            pltpu.VMEM((top, rows), jnp.int32),
            pltpu.VMEM((top, rows), F32),
            pltpu.SemaphoreType.DMA((3,)),
        ],
        8,
        rows * room,
        4 * rows * width,
    )

    def along(k):
        return [(s, ((s // PAIR + k) % places) * PAIR + s % PAIR) for s in range(n_expert)]

    def across(k):
        return [(s, (s + k) % n_blk) for s in range(n_blk)]

    def across_other(k):
        return [
            (s * n_blk + b, (s ^ 1) * n_blk + (b + k) % n_blk)
            for s in range(n_expert)
            for b in range(n_blk)
        ]

    swap = [(s, s ^ 1) for s in range(n_expert)]

    kb = largest_step(width, (512, 384, 256, 128))
    per = width // kb
    steps = per * (n_blk - 1)
    first_held, second_held, third_held = min(2, per), min(2, steps), min(3, steps)

    def blocks(count):
        return pltpu.VMEM((count, hid, kb), BF16)

    held = call(
        functools.partial(head_kernel, first_held, per),
        [blocks(first_held)] * 2,
        (packed, w_gate, w_up),
        (hbm,) * 3,
        [pltpu.SemaphoreType.DMA((2, first_held))],
        4,
        0,
        4 * hid * kb * first_held,
    )
    pieces = [packed] + [lax.ppermute(packed, "expert", along(k)) for k in range(1, places)]
    pieces, held = lax.optimization_barrier((pieces, held))
    own = jnp.concatenate(pieces, axis=0)
    other = lax.ppermute(own, "expert", swap)
    bare = own[:, :width]
    sent = []
    for j in range(1, n_blk):
        sent.append(lax.ppermute(bare, "blk", across(-j)))
        sent.append(lax.ppermute(bare, ("expert", "blk"), across_other(-j)))

    sums = [jax.ShapeDtypeStruct((hid, tokens_all), F32)] * 2

    def up(parts, held, more, last, outs, operands):
        weights = (w_gate, w_up, w_down) if last else (w_gate, w_up)
        return call(
            functools.partial(up_kernel, kb, parts, held, more, last),
            outs,
            (*operands, *weights),
            (vmem,) * len(operands) + (hbm,) * len(weights),
            [
                pltpu.VMEM((width * len(parts), tokens_all), BF16),
                blocks(SLOTS),
                blocks(SLOTS),
                pltpu.SemaphoreType.DMA((2, SLOTS)),
                pltpu.SemaphoreType.DMA((2, more)),
            ]
            + [pltpu.VMEM(each.shape, F32) for each in sums if last],
            23 if last else 20,
            4 * tokens_all * hid * width * len(parts),
            4 * hid * width * len(parts),
        )

    *partial_sums, gate_held, up_held = up(
        (0,), first_held, second_held, False, sums + [blocks(second_held)] * 2, (own, other, *held)
    )
    hidden, down_held = up(
        tuple(range(1, n_blk)),
        second_held,
        third_held,
        True,
        [jax.ShapeDtypeStruct((tokens_all, hid), BF16), blocks(third_held)],
        (*sent, *partial_sums, gate_held, up_held),
    )

    def down(hidden, first, count, more, *down_held):
        held = down_held[0].shape[0] if down_held else 0
        span = min(count, per)
        shape = (count // span, half, span * kb)
        return call(
            functools.partial(down_kernel, width, first, count, held, more, experts, shares),
            [jax.ShapeDtypeStruct(shape, F32), jax.ShapeDtypeStruct(shape, BF16)] + [blocks(more)] * (more > 0),
            (hidden, own, other, *down_held, w_down),
            (vmem,) * (3 + len(down_held)) + (hbm,),
            [
                blocks(min(SLOTS, max(count - held, 1))),
                pltpu.SemaphoreType.DMA((SLOTS,)),
                pltpu.SemaphoreType.DMA((max(more, 1),)),
            ],
            14,
            2 * tokens_all * hid * kb * count,
            2 * hid * kb * count,
        )

    early = per // 3
    away, given, *early_held = down(hidden, per, steps, early, down_held)
    given = lax.ppermute(given, "expert", swap)
    parts = [down(hidden, 0, early, 0, *early_held)] if early else []
    away = (away + given.astype(F32)).astype(BF16)
    away, hidden = lax.optimization_barrier((away, hidden))
    away = jnp.pad(away, ((0, 0), (0, 0), (0, room)))
    total = [lax.ppermute(away[j - 1], "blk", across(j))[:, :width] for j in range(1, n_blk)]
    parts.append(down(hidden, early, per - early, 0))
    kept, given = (jnp.concatenate([part[at][0] for part in parts], axis=1) for at in range(2))
    summed = kept + lax.ppermute(given, "expert", swap).astype(F32)
    for term in total:
        summed = summed + term.astype(F32)
    mixed = summed[:rows]
    for k in range(1, places):
        piece = summed[k * rows : (k + 1) * rows].astype(BF16)
        mixed = mixed + lax.ppermute(piece, "expert", along(-k)).astype(F32)
    return mixed.astype(BF16)


def solution(mesh):
    placed = (
        P(("groups", "expert"), "blk"),
        P(("groups", "expert"), None),
        P(("groups", "expert"), None),
        P("expert", "blk", None),
        P("expert", "blk", None),
        P("expert", "blk", None),
    )
    return jax.shard_map(
        body, mesh=mesh, in_specs=placed, out_specs=P(("groups", "expert"), "blk"), check_vma=False
    )
```

```python
import functools

import jax
import jax.numpy as jnp
from jax import lax
from jax.experimental import pallas as pl
from jax.experimental.pallas import tpu as pltpu
from jax.sharding import PartitionSpec as P

FFW = 5376
PAIR = 2
LANES = 128
SLOTS = 3
MIB = 1024 * 1024
F32 = jnp.float32
BF16 = jnp.bfloat16


def largest_step(total, choices):
    for step in choices:
        if total % step == 0:
            return step
    return total


def call(kernel, outs, operands, spaces, scratch, limit, flops, moved):
    return pl.pallas_call(
        kernel,
        out_shape=outs,
        in_specs=[pl.BlockSpec(memory_space=space) for space in spaces],
        out_specs=[pl.BlockSpec(memory_space=pltpu.VMEM) for unused in outs],
        scratch_shapes=scratch,
        compiler_params=pltpu.CompilerParams(vmem_limit_bytes=limit * MIB),
        cost_estimate=pl.CostEstimate(flops=flops, bytes_accessed=moved, transcendentals=0),
    )(*operands)


def in_hbm(*arrays):
    return [pltpu.with_memory_space_constraint(array, pltpu.HBM) for array in arrays]


def columns_of(step, per, block):
    owner = lax.rem(lax.axis_index("blk") + step // per, lax.axis_size("blk"))
    return pl.ds(pl.multiple_of((owner * per + lax.rem(step, per)) * block, LANES), block)


def moves(weights, step, per, targets, sems):
    return [
        pltpu.make_async_copy(weight.at[0, :, columns_of(step, per, target.shape[-1])], target, sem)
        for weight, target, sem in zip(weights, targets, sems)
    ]


def stream(held, count, fetch, ahead, begin, from_held, from_ring):
    rest = count - held
    for at in range(min(SLOTS, rest)):
        for copy in fetch(held + at, at):
            copy.start()
    if rest == 0:
        for copy in ahead:
            copy.start()
    begin()

    def first(step, carry):
        from_held(step)
        return carry

    if held:
        lax.fori_loop(0, held, first, 0)

    def then(at, carry):
        later = at + SLOTS - 1

        @pl.when((at > 0) & (later < rest))
        def _():
            for copy in fetch(held + later, lax.rem(later, SLOTS)):
                copy.start()

        @pl.when(at == max(rest - SLOTS, 0))
        def _():
            for copy in ahead:
                copy.start()

        slot = lax.rem(at, SLOTS)
        from_ring(held + at, slot, fetch(held + at, slot))
        return carry

    if rest:
        lax.fori_loop(0, rest, then, 0)


def finish(copies):
    for copy in copies:
        copy.wait()


def head_kernel(count, per, after, w_gate, w_up, gate, up, sems):
    copies = []
    for step in range(count):
        at = (sems.at[0, step], sems.at[1, step])
        copies += moves((w_gate, w_up), step, per, (gate.at[step], up.at[step]), at)
    for copy in copies:
        copy.start()
    finish(copies)


def pack_kernel(experts, tokens, ids, weights, out, held, named, weighed, sems):
    copies = [
        pltpu.make_async_copy(source, target, sems.at[at])
        for at, (source, target) in enumerate(((ids, named), (weights, weighed), (tokens, held)))
    ]
    for copy in copies:
        copy.start()
    rows, width = tokens.shape
    shape = (rows, out.shape[1] - width)
    lane = lax.broadcasted_iota(jnp.int32, shape, 1)
    diagonal = lax.broadcasted_iota(jnp.int32, (rows, rows), 0) == lax.broadcasted_iota(
        jnp.int32, (rows, rows), 1
    )
    coef = jnp.zeros(shape, F32)
    copies[0].wait()
    copies[1].wait()
    for k in range(ids.shape[0]):
        name = jnp.sum(jnp.where(diagonal, named[k : k + 1], 0), axis=1, keepdims=True)
        weight = jnp.sum(jnp.where(diagonal, weighed[k : k + 1], 0.0), axis=1, keepdims=True)
        coef += jnp.where(lax.rem(lane, experts) == name, weight, 0.0)
    high = coef.astype(BF16).astype(F32)
    middle = (coef - high).astype(BF16).astype(F32)
    low = coef - high - middle
    part = jnp.where(lane < experts, high, jnp.where(lane < 2 * experts, middle, low))
    out[:, width:] = jnp.where(lane < 3 * experts, part, 0.0).astype(BF16)
    copies[2].wait()
    out[:, :width] = held[...]


def up_kernel(kb, parts, held, more, last, *refs):
    sent, refs = refs[: 2 * len(parts)], refs[2 * len(parts) :]
    earlier, refs = (refs[:2], refs[2:]) if last else ((), refs)
    (gate_held, up_held, w_gate, w_up), refs = refs[:4], refs[4:]
    if last:
        w_down, hidden, down_next, x, gate_ring, up_ring, sems, next_sems, gate_sum, up_sum = refs
    else:
        gate_sum, up_sum, gate_next, up_next, x, gate_ring, up_ring, sems, next_sems = refs
    hid = w_gate.shape[1]
    width = x.shape[0] // len(parts)
    per = width // kb
    start = parts[0] * per
    weights = (w_gate, w_up)

    def fetch(step, slot):
        places = (gate_ring.at[slot], up_ring.at[slot])
        return moves(weights, start + step, per, places, (sems.at[0, slot], sems.at[1, slot]))

    ahead = []
    for k in range(more):
        if last:
            down_per = width // down_next.shape[-1]
            ahead += moves((w_down,), down_per + k, down_per, (down_next.at[k],), (next_sems.at[0, k],))
        else:
            places = (gate_next.at[k], up_next.at[k])
            at = (next_sems.at[0, k], next_sems.at[1, k])
            ahead += moves(weights, start + per + k, per, places, at)

    def begin():
        for j in range(len(parts)):
            rows = [sent[2 * j + at][:, :width].astype(F32) for at in range(2)]
            x[j * width : (j + 1) * width] = jnp.concatenate(rows, axis=0).T.astype(BF16)
        gate_sum[...] = earlier[0][...] if last else jnp.zeros_like(gate_sum)
        up_sum[...] = earlier[1][...] if last else jnp.zeros_like(up_sum)

    pass_width = kb if last or kb % 256 else 256

    def add(total, block, step):
        for first in range(0, kb, pass_width):
            right = x[pl.ds(pl.multiple_of(step * kb + first, LANES), pass_width)]
            left = block[:, first : first + pass_width]
            total[...] += jnp.dot(left, right, preferred_element_type=F32)

    def from_held(step):
        add(gate_sum, gate_held.at[step], step)
        add(up_sum, up_held.at[step], step)

    def from_ring(step, slot, waits):
        waits[0].wait()
        add(gate_sum, gate_ring.at[slot], step)
        waits[1].wait()
        add(up_sum, up_ring.at[slot], step)

    stream(held, len(parts) * per, fetch, ahead, begin, from_held, from_ring)
    if last:
        unit = largest_step(hid, (384,))
        for first in range(0, hid, unit):
            units = pl.ds(first, unit)
            gate = gate_sum[units]
            value = gate / (1.0 + jnp.exp(-gate)) * up_sum[units]
            hidden[:, units] = value.T.astype(BF16)
    finish(ahead)


def down_kernel(width, start, count, held, more, experts, shares, hidden, own, other, *refs):
    down_held, refs = (refs[0], refs[1:]) if held else (None, refs)
    w_down, *outs, ring, sems, next_sems = refs
    down_next = outs.pop() if more else None
    unused, half, span = outs[0].shape
    fb = ring.shape[-1]
    per, inside = width // fb, span // fb
    expert = lax.axis_index("expert") // shares
    packed = jnp.concatenate([own[:, width:], other[:, width:]], axis=0).astype(F32)
    lane = lax.broadcasted_iota(jnp.int32, packed.shape, 1)
    mine = (lax.rem(lane, experts) == expert) & (lane < 3 * experts)
    coef = jnp.sum(jnp.where(mine, packed, 0.0), axis=1, keepdims=True)

    def fetch(step, slot):
        return moves((w_down,), start + step, per, (ring.at[slot],), (sems.at[slot],))

    def put(step, block):
        value = jnp.dot(hidden[...], block, preferred_element_type=F32) * coef
        columns = pl.ds(pl.multiple_of(lax.rem(step, inside) * fb, LANES), fb)
        for at, out in enumerate(outs):
            out[step // inside, :, columns] = value[at * half : (at + 1) * half].astype(out.dtype)

    def from_held(step):
        put(step, down_held[step])

    def from_ring(step, slot, waits):
        waits[0].wait()
        put(step, ring[slot])

    ahead = []
    for k in range(more):
        ahead += moves((w_down,), k, per, (down_next.at[k],), (next_sems.at[k],))
    stream(held, count, fetch, ahead, lambda: None, from_held, from_ring)
    finish(ahead)


def body(tokens, expert_ids, route_weight, w_gate, w_up, w_down):
    n_expert = lax.axis_size("expert")
    n_blk = lax.axis_size("blk")
    rows, width = tokens.shape
    top = expert_ids.shape[1]
    hid = w_gate.shape[1]
    shares = FFW // (hid * n_blk)
    experts = n_expert // shares
    places = n_expert // PAIR
    half = places * rows
    tokens_all = PAIR * half
    room = -(-3 * experts // LANES) * LANES
    vmem, hbm = pltpu.VMEM, pl.ANY
    w_gate, w_up, w_down = in_hbm(w_gate, w_up, w_down)

    (packed,) = call(
        functools.partial(pack_kernel, experts),
        [jax.ShapeDtypeStruct((rows, width + room), BF16)],
        in_hbm(tokens, expert_ids.T, route_weight.T),
        (hbm,) * 3,
        [
            pltpu.VMEM((rows, width), BF16),
            pltpu.VMEM((top, rows), jnp.int32),
            pltpu.VMEM((top, rows), F32),
            pltpu.SemaphoreType.DMA((3,)),
        ],
        8,
        rows * room,
        4 * rows * width,
    )

    def along(k):
        return [(s, (s // PAIR ^ k) * PAIR + s % PAIR) for s in range(n_expert)]

    def across(k):
        return [(s, (s + k) % n_blk) for s in range(n_blk)]

    def across_other(k):
        return [
            (s * n_blk + b, (s ^ 1) * n_blk + (b + k) % n_blk)
            for s in range(n_expert)
            for b in range(n_blk)
        ]

    swap = [(s, s ^ 1) for s in range(n_expert)]

    kb = largest_step(width, (512, 384, 256, 128))
    per = width // kb
    steps = per * (n_blk - 1)
    first_held, second_held, third_held = min(2, per), min(1, steps), min(3, steps)

    def blocks(count):
        return pltpu.VMEM((count, hid, kb), BF16)

    held = call(
        functools.partial(head_kernel, first_held, per),
        [blocks(first_held)] * 2,
        (packed, w_gate, w_up),
        (hbm,) * 3,
        [pltpu.SemaphoreType.DMA((2, first_held))],
        4,
        0,
        4 * hid * kb * first_held,
    )
    pieces = [packed] + [lax.ppermute(packed, "expert", along(k)) for k in range(1, places)]
    pieces, held = lax.optimization_barrier((pieces, held))
    own = jnp.concatenate(pieces, axis=0)
    other = lax.ppermute(own, "expert", swap)
    bare = own[:, :width]
    sent = []
    for j in range(1, n_blk):
        sent.append(lax.ppermute(bare, "blk", across(-j)))
        sent.append(lax.ppermute(bare, ("expert", "blk"), across_other(-j)))

    sums = [jax.ShapeDtypeStruct((hid, tokens_all), F32)] * 2

    def up(parts, held, more, last, outs, operands):
        weights = (w_gate, w_up, w_down) if last else (w_gate, w_up)
        return call(
            functools.partial(up_kernel, kb, parts, held, more, last),
            outs,
            (*operands, *weights),
            (vmem,) * len(operands) + (hbm,) * len(weights),
            [
                pltpu.VMEM((width * len(parts), tokens_all), BF16),
                blocks(SLOTS),
                blocks(SLOTS),
                pltpu.SemaphoreType.DMA((2, SLOTS)),
                pltpu.SemaphoreType.DMA((2, more)),
            ]
            + [pltpu.VMEM(each.shape, F32) for each in sums if last],
            23 if last else 20,
            4 * tokens_all * hid * width * len(parts),
            4 * hid * width * len(parts),
        )

    *partial_sums, gate_held, up_held = up(
        (0,), first_held, second_held, False, sums + [blocks(second_held)] * 2, (own, other, *held)
    )
    hidden, down_held = up(
        tuple(range(1, n_blk)),
        second_held,
        third_held,
        True,
        [jax.ShapeDtypeStruct((tokens_all, hid), BF16), blocks(third_held)],
        (*sent, *partial_sums, gate_held, up_held),
    )

    def down(hidden, first, count, more, *down_held):
        held = down_held[0].shape[0] if down_held else 0
        span = min(count, per)
        shape = (count // span, half, span * kb)
        return call(
            functools.partial(down_kernel, width, first, count, held, more, experts, shares),
            [jax.ShapeDtypeStruct(shape, F32), jax.ShapeDtypeStruct(shape, BF16)] + [blocks(more)] * (more > 0),
            (hidden, own, other, *down_held, w_down),
            (vmem,) * (3 + len(down_held)) + (hbm,),
            [
                blocks(min(SLOTS, max(count - held, 1))),
                pltpu.SemaphoreType.DMA((SLOTS,)),
                pltpu.SemaphoreType.DMA((max(more, 1),)),
            ],
            14,
            2 * tokens_all * hid * kb * count,
            2 * hid * kb * count,
        )

    early = per // 3
    away, given, *early_held = down(hidden, per, steps, early, down_held)
    given = lax.ppermute(given, "expert", swap)
    parts = [down(hidden, 0, early, 0, *early_held)] if early else []
    away = (away + given.astype(F32)).astype(BF16)
    away, hidden = lax.optimization_barrier((away, hidden))
    away = jnp.pad(away, ((0, 0), (0, 0), (0, room)))
    total = [lax.ppermute(away[j - 1], "blk", across(j))[:, :width] for j in range(1, n_blk)]
    parts.append(down(hidden, early, per - early, 0))
    kept, given = (jnp.concatenate([part[at][0] for part in parts], axis=1) for at in range(2))
    summed = kept + lax.ppermute(given, "expert", swap).astype(F32)
    for term in total:
        summed = summed + term.astype(F32)
    mixed = summed[:rows]
    for k in range(1, places):
        piece = summed[k * rows : (k + 1) * rows].astype(BF16)
        mixed = mixed + lax.ppermute(piece, "expert", along(k)).astype(F32)
    return mixed.astype(BF16)


def solution(mesh):
    placed = (
        P(("groups", "expert"), "blk"),
        P(("groups", "expert"), None),
        P(("groups", "expert"), None),
        P("expert", "blk", None),
        P("expert", "blk", None),
        P("expert", "blk", None),
    )
    return jax.shard_map(
        body, mesh=mesh, in_specs=placed, out_specs=P(("groups", "expert"), "blk"), check_vma=False
    )
```

```python
import functools

import jax
import jax.numpy as jnp
from jax import lax
from jax.experimental import pallas as pl
from jax.experimental.pallas import tpu as pltpu
from jax.sharding import PartitionSpec as P

FFW = 5376
PAIR = 2
LANES = 128
SLOTS = 3
MIB = 1024 * 1024
F32 = jnp.float32
BF16 = jnp.bfloat16


def largest_step(total, choices):
    for step in choices:
        if total % step == 0:
            return step
    return total


def call(kernel, outs, operands, spaces, scratch, limit, flops, moved):
    return pl.pallas_call(
        kernel,
        out_shape=outs,
        in_specs=[pl.BlockSpec(memory_space=space) for space in spaces],
        out_specs=[pl.BlockSpec(memory_space=pltpu.VMEM) for unused in outs],
        scratch_shapes=scratch,
        compiler_params=pltpu.CompilerParams(vmem_limit_bytes=limit * MIB),
        cost_estimate=pl.CostEstimate(flops=flops, bytes_accessed=moved, transcendentals=0),
    )(*operands)


def in_hbm(*arrays):
    return [pltpu.with_memory_space_constraint(array, pltpu.HBM) for array in arrays]


def columns_of(step, per, block):
    owner = lax.rem(lax.axis_index("blk") + step // per, lax.axis_size("blk"))
    return pl.ds(pl.multiple_of((owner * per + lax.rem(step, per)) * block, LANES), block)


def moves(weights, step, per, targets, sems):
    return [
        pltpu.make_async_copy(weight.at[0, :, columns_of(step, per, target.shape[-1])], target, sem)
        for weight, target, sem in zip(weights, targets, sems)
    ]


def stream(held, count, fetch, ahead, begin, from_held, from_ring):
    rest = count - held
    lead = held if held and rest <= SLOTS else SLOTS - 1
    first_ahead = min(max(count - lead, 0), count - 1)
    second_ahead = min(first_ahead + 1, count - 1)
    several = -(-len(ahead) // 2)
    for at in range(min(lead - held + 1, rest)):
        for copy in fetch(held + at, at):
            copy.start()
    begin()

    def issue(step):
        at = step + lead - held
        if rest:

            @pl.when((step > 0) & (at >= 0) & (at < rest))
            def _():
                for copy in fetch(held + at, lax.rem(at, SLOTS)):
                    copy.start()

        if ahead:

            @pl.when(step == first_ahead)
            def _():
                for copy in ahead[:several]:
                    copy.start()

            @pl.when(step == second_ahead)
            def _():
                for copy in ahead[several:]:
                    copy.start()

    def first(step, carry):
        issue(step)
        from_held(step)
        return carry

    if held:
        lax.fori_loop(0, held, first, 0)

    def then(at, carry):
        issue(held + at)
        slot = lax.rem(at, SLOTS)
        from_ring(held + at, slot, fetch(held + at, slot))
        return carry

    if rest:
        lax.fori_loop(0, rest, then, 0)


def finish(copies):
    for copy in copies:
        copy.wait()


def head_kernel(count, per, after, w_gate, w_up, gate, up, sems):
    copies = []
    for step in range(count):
        at = (sems.at[0, step], sems.at[1, step])
        copies += moves((w_gate, w_up), step, per, (gate.at[step], up.at[step]), at)
    for copy in copies:
        copy.start()
    finish(copies)


def pack_kernel(experts, tokens, ids, weights, out, held, named, weighed, sems):
    copies = [
        pltpu.make_async_copy(source, target, sems.at[at])
        for at, (source, target) in enumerate(((ids, named), (weights, weighed), (tokens, held)))
    ]
    for copy in copies:
        copy.start()
    rows, width = tokens.shape
    shape = (rows, out.shape[1] - width)
    lane = lax.broadcasted_iota(jnp.int32, shape, 1)
    diagonal = lax.broadcasted_iota(jnp.int32, (rows, rows), 0) == lax.broadcasted_iota(
        jnp.int32, (rows, rows), 1
    )
    coef = jnp.zeros(shape, F32)
    copies[0].wait()
    copies[1].wait()
    for k in range(ids.shape[0]):
        name = jnp.sum(jnp.where(diagonal, named[k : k + 1], 0), axis=1, keepdims=True)
        weight = jnp.sum(jnp.where(diagonal, weighed[k : k + 1], 0.0), axis=1, keepdims=True)
        coef += jnp.where(lax.rem(lane, experts) == name, weight, 0.0)
    high = coef.astype(BF16).astype(F32)
    middle = (coef - high).astype(BF16).astype(F32)
    low = coef - high - middle
    part = jnp.where(lane < experts, high, jnp.where(lane < 2 * experts, middle, low))
    out[:, width:] = jnp.where(lane < 3 * experts, part, 0.0).astype(BF16)
    copies[2].wait()
    out[:, :width] = held[...]


def up_kernel(kb, parts, held, more, last, *refs):
    sent, refs = refs[: 2 * len(parts)], refs[2 * len(parts) :]
    earlier, refs = (refs[:2], refs[2:]) if last else ((), refs)
    (gate_held, up_held, w_gate, w_up), refs = refs[:4], refs[4:]
    if last:
        w_down, hidden, down_next, x, gate_ring, up_ring, sems, next_sems, gate_sum, up_sum = refs
    else:
        gate_sum, up_sum, gate_next, up_next, x, gate_ring, up_ring, sems, next_sems = refs
    hid = w_gate.shape[1]
    width = x.shape[0] // len(parts)
    per = width // kb
    start = parts[0] * per
    weights = (w_gate, w_up)

    def fetch(step, slot):
        places = (gate_ring.at[slot], up_ring.at[slot])
        return moves(weights, start + step, per, places, (sems.at[0, slot], sems.at[1, slot]))

    ahead = []
    for k in range(more):
        if last:
            down_per = width // down_next.shape[-1]
            ahead += moves((w_down,), down_per + k, down_per, (down_next.at[k],), (next_sems.at[0, k],))
        else:
            places = (gate_next.at[k], up_next.at[k])
            at = (next_sems.at[0, k], next_sems.at[1, k])
            ahead += moves(weights, start + per + k, per, places, at)

    def begin():
        for j in range(len(parts)):
            rows = [sent[2 * j + at][:, :width].astype(F32) for at in range(2)]
            x[j * width : (j + 1) * width] = jnp.concatenate(rows, axis=0).T.astype(BF16)
        gate_sum[...] = earlier[0][...] if last else jnp.zeros_like(gate_sum)
        up_sum[...] = earlier[1][...] if last else jnp.zeros_like(up_sum)

    def right(step):
        return x[pl.ds(pl.multiple_of(step * kb, LANES), kb)]

    def from_held(step):
        gate_sum[...] += jnp.dot(gate_held[step], right(step), preferred_element_type=F32)
        up_sum[...] += jnp.dot(up_held[step], right(step), preferred_element_type=F32)

    def from_ring(step, slot, waits):
        waits[0].wait()
        gate_sum[...] += jnp.dot(gate_ring[slot], right(step), preferred_element_type=F32)
        waits[1].wait()
        up_sum[...] += jnp.dot(up_ring[slot], right(step), preferred_element_type=F32)

    stream(held, len(parts) * per, fetch, ahead, begin, from_held, from_ring)
    if last:
        unit = largest_step(hid, (384,))
        for first in range(0, hid, unit):
            units = pl.ds(first, unit)
            gate = gate_sum[units]
            value = gate / (1.0 + jnp.exp(-gate)) * up_sum[units]
            hidden[:, units] = value.T.astype(BF16)
    finish(ahead)


def down_kernel(width, start, count, held, more, experts, shares, hidden, own, other, *refs):
    down_held, refs = (refs[0], refs[1:]) if held else (None, refs)
    w_down, *outs, ring, sems, next_sems = refs
    down_next = outs.pop() if more else None
    unused, half, span = outs[0].shape
    fb = ring.shape[-1]
    per, inside = width // fb, span // fb
    expert = lax.axis_index("expert") // shares
    packed = jnp.concatenate([own[:, width:], other[:, width:]], axis=0).astype(F32)
    lane = lax.broadcasted_iota(jnp.int32, packed.shape, 1)
    mine = (lax.rem(lane, experts) == expert) & (lane < 3 * experts)
    coef = jnp.sum(jnp.where(mine, packed, 0.0), axis=1, keepdims=True)

    def fetch(step, slot):
        return moves((w_down,), start + step, per, (ring.at[slot],), (sems.at[slot],))

    def put(step, block):
        value = jnp.dot(hidden[...], block, preferred_element_type=F32) * coef
        columns = pl.ds(pl.multiple_of(lax.rem(step, inside) * fb, LANES), fb)
        for at, out in enumerate(outs):
            out[step // inside, :, columns] = value[at * half : (at + 1) * half].astype(out.dtype)

    def from_held(step):
        put(step, down_held[step])

    def from_ring(step, slot, waits):
        waits[0].wait()
        put(step, ring[slot])

    ahead = []
    for k in range(more):
        ahead += moves((w_down,), k, per, (down_next.at[k],), (next_sems.at[k],))
    stream(held, count, fetch, ahead, lambda: None, from_held, from_ring)
    finish(ahead)


def body(tokens, expert_ids, route_weight, w_gate, w_up, w_down):
    n_expert = lax.axis_size("expert")
    n_blk = lax.axis_size("blk")
    rows, width = tokens.shape
    top = expert_ids.shape[1]
    hid = w_gate.shape[1]
    shares = FFW // (hid * n_blk)
    experts = n_expert // shares
    places = n_expert // PAIR
    half = places * rows
    tokens_all = PAIR * half
    room = -(-3 * experts // LANES) * LANES
    vmem, hbm = pltpu.VMEM, pl.ANY
    w_gate, w_up, w_down = in_hbm(w_gate, w_up, w_down)

    (packed,) = call(
        functools.partial(pack_kernel, experts),
        [jax.ShapeDtypeStruct((rows, width + room), BF16)],
        in_hbm(tokens, expert_ids.T, route_weight.T),
        (hbm,) * 3,
        [
            pltpu.VMEM((rows, width), BF16),
            pltpu.VMEM((top, rows), jnp.int32),
            pltpu.VMEM((top, rows), F32),
            pltpu.SemaphoreType.DMA((3,)),
        ],
        8,
        rows * room,
        4 * rows * width,
    )

    def along(k):
        return [(s, ((s // PAIR + k) % places) * PAIR + s % PAIR) for s in range(n_expert)]

    def across(k):
        return [(s, (s + k) % n_blk) for s in range(n_blk)]

    def across_other(k):
        return [
            (s * n_blk + b, (s ^ 1) * n_blk + (b + k) % n_blk)
            for s in range(n_expert)
            for b in range(n_blk)
        ]

    swap = [(s, s ^ 1) for s in range(n_expert)]

    kb = largest_step(width, (512, 384, 256, 128))
    per = width // kb
    steps = per * (n_blk - 1)
    first_held, second_held, third_held = min(2, per), min(2, steps), min(3, steps)

    def blocks(count):
        return pltpu.VMEM((count, hid, kb), BF16)

    held = call(
        functools.partial(head_kernel, first_held, per),
        [blocks(first_held)] * 2,
        (packed, w_gate, w_up),
        (hbm,) * 3,
        [pltpu.SemaphoreType.DMA((2, first_held))],
        4,
        0,
        4 * hid * kb * first_held,
    )
    pieces = [packed] + [lax.ppermute(packed, "expert", along(k)) for k in range(1, places)]
    pieces, held = lax.optimization_barrier((pieces, held))
    own = jnp.concatenate(pieces, axis=0)
    other = lax.ppermute(own, "expert", swap)
    bare = own[:, :width]
    sent = []
    for j in range(1, n_blk):
        sent.append(lax.ppermute(bare, "blk", across(-j)))
        sent.append(lax.ppermute(bare, ("expert", "blk"), across_other(-j)))

    sums = [jax.ShapeDtypeStruct((hid, tokens_all), F32)] * 2

    def up(parts, held, more, last, outs, operands):
        weights = (w_gate, w_up, w_down) if last else (w_gate, w_up)
        return call(
            functools.partial(up_kernel, kb, parts, held, more, last),
            outs,
            (*operands, *weights),
            (vmem,) * len(operands) + (hbm,) * len(weights),
            [
                pltpu.VMEM((width * len(parts), tokens_all), BF16),
                blocks(SLOTS),
                blocks(SLOTS),
                pltpu.SemaphoreType.DMA((2, SLOTS)),
                pltpu.SemaphoreType.DMA((2, more)),
            ]
            + [pltpu.VMEM(each.shape, F32) for each in sums if last],
            23 if last else 20,
            4 * tokens_all * hid * width * len(parts),
            4 * hid * width * len(parts),
        )

    *partial_sums, gate_held, up_held = up(
        (0,), first_held, second_held, False, sums + [blocks(second_held)] * 2, (own, other, *held)
    )
    hidden, down_held = up(
        tuple(range(1, n_blk)),
        second_held,
        third_held,
        True,
        [jax.ShapeDtypeStruct((tokens_all, hid), BF16), blocks(third_held)],
        (*sent, *partial_sums, gate_held, up_held),
    )

    def down(hidden, first, count, more, *down_held):
        held = down_held[0].shape[0] if down_held else 0
        span = min(count, per)
        shape = (count // span, half, span * kb)
        return call(
            functools.partial(down_kernel, width, first, count, held, more, experts, shares),
            [jax.ShapeDtypeStruct(shape, F32), jax.ShapeDtypeStruct(shape, BF16)] + [blocks(more)] * (more > 0),
            (hidden, own, other, *down_held, w_down),
            (vmem,) * (3 + len(down_held)) + (hbm,),
            [
                blocks(min(SLOTS, max(count - held, 1))),
                pltpu.SemaphoreType.DMA((SLOTS,)),
                pltpu.SemaphoreType.DMA((max(more, 1),)),
            ],
            14,
            2 * tokens_all * hid * kb * count,
            2 * hid * kb * count,
        )

    early = per // 3
    away, given, *early_held = down(hidden, per, steps, early, down_held)
    given = lax.ppermute(given, "expert", swap)
    parts = [down(hidden, 0, early, 0, *early_held)] if early else []
    away = (away + given.astype(F32)).astype(BF16)
    away, hidden = lax.optimization_barrier((away, hidden))
    away = jnp.pad(away, ((0, 0), (0, 0), (0, room)))
    total = [lax.ppermute(away[j - 1], "blk", across(j))[:, :width] for j in range(1, n_blk)]
    parts.append(down(hidden, early, per - early, 0))
    kept, given = (jnp.concatenate([part[at][0] for part in parts], axis=1) for at in range(2))
    summed = kept + lax.ppermute(given, "expert", swap).astype(F32)
    for term in total:
        summed = summed + term.astype(F32)
    mixed = summed[:rows]
    for k in range(1, places):
        piece = summed[k * rows : (k + 1) * rows].astype(BF16)
        mixed = mixed + lax.ppermute(piece, "expert", along(-k)).astype(F32)
    return mixed.astype(BF16)


def solution(mesh):
    placed = (
        P(("groups", "expert"), "blk"),
        P(("groups", "expert"), None),
        P(("groups", "expert"), None),
        P("expert", "blk", None),
        P("expert", "blk", None),
        P("expert", "blk", None),
    )
    return jax.shard_map(
        body, mesh=mesh, in_specs=placed, out_specs=P(("groups", "expert"), "blk"), check_vma=False
    )
```

```python
import functools

import jax
import jax.numpy as jnp
from jax import lax
from jax.experimental import pallas as pl
from jax.experimental.pallas import tpu as pltpu
from jax.sharding import PartitionSpec as P

FFW = 5376
PAIR = 2
LANES = 128
SLOTS = 3
MIB = 1024 * 1024
F32 = jnp.float32
BF16 = jnp.bfloat16


def largest_step(total, choices):
    for step in choices:
        if total % step == 0:
            return step
    return total


def call(kernel, outs, operands, spaces, scratch, limit, flops, moved):
    return pl.pallas_call(
        kernel,
        out_shape=outs,
        in_specs=[pl.BlockSpec(memory_space=space) for space in spaces],
        out_specs=[pl.BlockSpec(memory_space=pltpu.VMEM) for unused in outs],
        scratch_shapes=scratch,
        compiler_params=pltpu.CompilerParams(vmem_limit_bytes=limit * MIB),
        cost_estimate=pl.CostEstimate(flops=flops, bytes_accessed=moved, transcendentals=0),
    )(*operands)


def in_hbm(*arrays):
    return [pltpu.with_memory_space_constraint(array, pltpu.HBM) for array in arrays]


def columns_of(step, per, block):
    owner = lax.rem(lax.axis_index("blk") + step // per, lax.axis_size("blk"))
    return pl.ds(pl.multiple_of((owner * per + lax.rem(step, per)) * block, LANES), block)


def moves(weights, step, per, targets, sems):
    return [
        pltpu.make_async_copy(weight.at[0, :, columns_of(step, per, target.shape[-1])], target, sem)
        for weight, target, sem in zip(weights, targets, sems)
    ]


def stream(held, count, fetch, ahead, begin, from_held, from_ring):
    rest = count - held
    for at in range(min(SLOTS, rest)):
        for copy in fetch(held + at, at):
            copy.start()
    if rest == 0:
        for copy in ahead:
            copy.start()
    begin()

    def first(step, carry):
        from_held(step)
        return carry

    if held:
        lax.fori_loop(0, held, first, 0)

    def then(at, carry):
        later = at + SLOTS - 1

        @pl.when((at > 0) & (later < rest))
        def _():
            for copy in fetch(held + later, lax.rem(later, SLOTS)):
                copy.start()

        def start_ahead():
            @pl.when(at == 0)
            def _():
                for copy in ahead:
                    copy.start()

        slot = lax.rem(at, SLOTS)
        waits = fetch(held + at, slot)
        if rest <= SLOTS:
            start_ahead()
        waits[0].wait()
        if rest > SLOTS:
            start_ahead()
        from_ring(held + at, slot, waits[1:])
        return carry

    if rest:
        lax.fori_loop(0, rest, then, 0)


def finish(copies):
    for copy in copies:
        copy.wait()


def head_kernel(count, per, after, w_gate, w_up, gate, up, sems):
    copies = []
    for step in range(count):
        at = (sems.at[0, step], sems.at[1, step])
        copies += moves((w_gate, w_up), step, per, (gate.at[step], up.at[step]), at)
    for copy in copies:
        copy.start()
    finish(copies)


def pack_kernel(experts, tokens, ids, weights, out, held, named, weighed, sems):
    copies = [
        pltpu.make_async_copy(source, target, sems.at[at])
        for at, (source, target) in enumerate(((ids, named), (weights, weighed), (tokens, held)))
    ]
    for copy in copies:
        copy.start()
    rows, width = tokens.shape
    shape = (rows, out.shape[1] - width)
    lane = lax.broadcasted_iota(jnp.int32, shape, 1)
    diagonal = lax.broadcasted_iota(jnp.int32, (rows, rows), 0) == lax.broadcasted_iota(
        jnp.int32, (rows, rows), 1
    )
    coef = jnp.zeros(shape, F32)
    copies[0].wait()
    copies[1].wait()
    for k in range(ids.shape[0]):
        name = jnp.sum(jnp.where(diagonal, named[k : k + 1], 0), axis=1, keepdims=True)
        weight = jnp.sum(jnp.where(diagonal, weighed[k : k + 1], 0.0), axis=1, keepdims=True)
        coef += jnp.where(lax.rem(lane, experts) == name, weight, 0.0)
    high = coef.astype(BF16).astype(F32)
    middle = (coef - high).astype(BF16).astype(F32)
    low = coef - high - middle
    part = jnp.where(lane < experts, high, jnp.where(lane < 2 * experts, middle, low))
    out[:, width:] = jnp.where(lane < 3 * experts, part, 0.0).astype(BF16)
    copies[2].wait()
    out[:, :width] = held[...]


def up_kernel(kb, parts, held, more, last, *refs):
    sent, refs = refs[: 2 * len(parts)], refs[2 * len(parts) :]
    earlier, refs = (refs[:2], refs[2:]) if last else ((), refs)
    (gate_held, up_held, w_gate, w_up), refs = refs[:4], refs[4:]
    if last:
        w_down, hidden, down_next, x, gate_ring, up_ring, sems, next_sems, gate_sum, up_sum = refs
    else:
        gate_sum, up_sum, gate_next, up_next, x, gate_ring, up_ring, sems, next_sems = refs
    hid = w_gate.shape[1]
    width = x.shape[0] // len(parts)
    per = width // kb
    start = parts[0] * per
    weights = (w_gate, w_up)

    def fetch(step, slot):
        places = (gate_ring.at[slot], up_ring.at[slot])
        return moves(weights, start + step, per, places, (sems.at[0, slot], sems.at[1, slot]))

    ahead = []
    for k in range(more):
        if last:
            down_per = width // down_next.shape[-1]
            ahead += moves((w_down,), down_per + k, down_per, (down_next.at[k],), (next_sems.at[0, k],))
        else:
            places = (gate_next.at[k], up_next.at[k])
            at = (next_sems.at[0, k], next_sems.at[1, k])
            ahead += moves(weights, start + per + k, per, places, at)

    def begin():
        for j in range(len(parts)):
            rows = [sent[2 * j + at][:, :width].astype(F32) for at in range(2)]
            x[j * width : (j + 1) * width] = jnp.concatenate(rows, axis=0).T.astype(BF16)
        gate_sum[...] = earlier[0][...] if last else jnp.zeros_like(gate_sum)
        up_sum[...] = earlier[1][...] if last else jnp.zeros_like(up_sum)

    def right(step):
        return x[pl.ds(pl.multiple_of(step * kb, LANES), kb)]

    def from_held(step):
        gate_sum[...] += jnp.dot(gate_held[step], right(step), preferred_element_type=F32)
        up_sum[...] += jnp.dot(up_held[step], right(step), preferred_element_type=F32)

    def from_ring(step, slot, waits):
        gate_sum[...] += jnp.dot(gate_ring[slot], right(step), preferred_element_type=F32)
        waits[0].wait()
        up_sum[...] += jnp.dot(up_ring[slot], right(step), preferred_element_type=F32)

    stream(held, len(parts) * per, fetch, ahead, begin, from_held, from_ring)
    if last:
        unit = largest_step(hid, (384,))
        for first in range(0, hid, unit):
            units = pl.ds(first, unit)
            gate = gate_sum[units]
            value = gate / (1.0 + jnp.exp(-gate)) * up_sum[units]
            hidden[:, units] = value.T.astype(BF16)
    finish(ahead)


def down_kernel(width, start, count, held, more, experts, shares, hidden, own, other, *refs):
    down_held, refs = (refs[0], refs[1:]) if held else (None, refs)
    w_down, *outs, ring, sems, next_sems = refs
    down_next = outs.pop() if more else None
    unused, half, span = outs[0].shape
    fb = ring.shape[-1]
    per, inside = width // fb, span // fb
    expert = lax.axis_index("expert") // shares
    packed = jnp.concatenate([own[:, width:], other[:, width:]], axis=0).astype(F32)
    lane = lax.broadcasted_iota(jnp.int32, packed.shape, 1)
    mine = (lax.rem(lane, experts) == expert) & (lane < 3 * experts)
    coef = jnp.sum(jnp.where(mine, packed, 0.0), axis=1, keepdims=True)

    def fetch(step, slot):
        return moves((w_down,), start + step, per, (ring.at[slot],), (sems.at[slot],))

    def put(step, block):
        value = jnp.dot(hidden[...], block, preferred_element_type=F32) * coef
        columns = pl.ds(pl.multiple_of(lax.rem(step, inside) * fb, LANES), fb)
        for at, out in enumerate(outs):
            out[step // inside, :, columns] = value[at * half : (at + 1) * half].astype(out.dtype)

    def from_held(step):
        put(step, down_held[step])

    def from_ring(step, slot, waits):
        put(step, ring[slot])

    ahead = []
    for k in range(more):
        ahead += moves((w_down,), k, per, (down_next.at[k],), (next_sems.at[k],))
    stream(held, count, fetch, ahead, lambda: None, from_held, from_ring)
    finish(ahead)


def body(tokens, expert_ids, route_weight, w_gate, w_up, w_down):
    n_expert = lax.axis_size("expert")
    n_blk = lax.axis_size("blk")
    rows, width = tokens.shape
    top = expert_ids.shape[1]
    hid = w_gate.shape[1]
    shares = FFW // (hid * n_blk)
    experts = n_expert // shares
    places = n_expert // PAIR
    half = places * rows
    tokens_all = PAIR * half
    room = -(-3 * experts // LANES) * LANES
    vmem, hbm = pltpu.VMEM, pl.ANY
    w_gate, w_up, w_down = in_hbm(w_gate, w_up, w_down)

    (packed,) = call(
        functools.partial(pack_kernel, experts),
        [jax.ShapeDtypeStruct((rows, width + room), BF16)],
        in_hbm(tokens, expert_ids.T, route_weight.T),
        (hbm,) * 3,
        [
            pltpu.VMEM((rows, width), BF16),
            pltpu.VMEM((top, rows), jnp.int32),
            pltpu.VMEM((top, rows), F32),
            pltpu.SemaphoreType.DMA((3,)),
        ],
        8,
        rows * room,
        4 * rows * width,
    )

    def along(k):
        return [(s, ((s // PAIR + k) % places) * PAIR + s % PAIR) for s in range(n_expert)]

    def across(k):
        return [(s, (s + k) % n_blk) for s in range(n_blk)]

    def across_other(k):
        return [
            (s * n_blk + b, (s ^ 1) * n_blk + (b + k) % n_blk)
            for s in range(n_expert)
            for b in range(n_blk)
        ]

    swap = [(s, s ^ 1) for s in range(n_expert)]

    kb = largest_step(width, (512, 384, 256, 128))
    per = width // kb
    steps = per * (n_blk - 1)
    first_held, second_held, third_held = min(2, per), min(2, steps), min(3, steps)

    def blocks(count):
        return pltpu.VMEM((count, hid, kb), BF16)

    held = call(
        functools.partial(head_kernel, first_held, per),
        [blocks(first_held)] * 2,
        (packed, w_gate, w_up),
        (hbm,) * 3,
        [pltpu.SemaphoreType.DMA((2, first_held))],
        4,
        0,
        4 * hid * kb * first_held,
    )
    pieces = [packed] + [lax.ppermute(packed, "expert", along(k)) for k in range(1, places)]
    pieces, held = lax.optimization_barrier((pieces, held))
    own = jnp.concatenate(pieces, axis=0)
    other = lax.ppermute(own, "expert", swap)
    bare = own[:, :width]
    sent = []
    for j in range(1, n_blk):
        sent.append(lax.ppermute(bare, "blk", across(-j)))
        sent.append(lax.ppermute(bare, ("expert", "blk"), across_other(-j)))

    sums = [jax.ShapeDtypeStruct((hid, tokens_all), F32)] * 2

    def up(parts, held, more, last, outs, operands):
        weights = (w_gate, w_up, w_down) if last else (w_gate, w_up)
        return call(
            functools.partial(up_kernel, kb, parts, held, more, last),
            outs,
            (*operands, *weights),
            (vmem,) * len(operands) + (hbm,) * len(weights),
            [
                pltpu.VMEM((width * len(parts), tokens_all), BF16),
                blocks(SLOTS),
                blocks(SLOTS),
                pltpu.SemaphoreType.DMA((2, SLOTS)),
                pltpu.SemaphoreType.DMA((2, more)),
            ]
            + [pltpu.VMEM(each.shape, F32) for each in sums if last],
            23 if last else 20,
            4 * tokens_all * hid * width * len(parts),
            4 * hid * width * len(parts),
        )

    *partial_sums, gate_held, up_held = up(
        (0,), first_held, second_held, False, sums + [blocks(second_held)] * 2, (own, other, *held)
    )
    hidden, down_held = up(
        tuple(range(1, n_blk)),
        second_held,
        third_held,
        True,
        [jax.ShapeDtypeStruct((tokens_all, hid), BF16), blocks(third_held)],
        (*sent, *partial_sums, gate_held, up_held),
    )

    def down(hidden, first, count, more, *down_held):
        held = down_held[0].shape[0] if down_held else 0
        span = min(count, per)
        shape = (count // span, half, span * kb)
        return call(
            functools.partial(down_kernel, width, first, count, held, more, experts, shares),
            [jax.ShapeDtypeStruct(shape, F32), jax.ShapeDtypeStruct(shape, BF16)] + [blocks(more)] * (more > 0),
            (hidden, own, other, *down_held, w_down),
            (vmem,) * (3 + len(down_held)) + (hbm,),
            [
                blocks(min(SLOTS, max(count - held, 1))),
                pltpu.SemaphoreType.DMA((SLOTS,)),
                pltpu.SemaphoreType.DMA((max(more, 1),)),
            ],
            14,
            2 * tokens_all * hid * kb * count,
            2 * hid * kb * count,
        )

    early = per // 3
    away, given, *early_held = down(hidden, per, steps, early, down_held)
    given = lax.ppermute(given, "expert", swap)
    parts = [down(hidden, 0, early, 0, *early_held)] if early else []
    away = (away + given.astype(F32)).astype(BF16)
    away, hidden = lax.optimization_barrier((away, hidden))
    away = jnp.pad(away, ((0, 0), (0, 0), (0, room)))
    total = [lax.ppermute(away[j - 1], "blk", across(j))[:, :width] for j in range(1, n_blk)]
    parts.append(down(hidden, early, per - early, 0))
    kept, given = (jnp.concatenate([part[at][0] for part in parts], axis=1) for at in range(2))
    summed = kept + lax.ppermute(given, "expert", swap).astype(F32)
    for term in total:
        summed = summed + term.astype(F32)
    mixed = summed[:rows]
    for k in range(1, places):
        piece = summed[k * rows : (k + 1) * rows].astype(BF16)
        mixed = mixed + lax.ppermute(piece, "expert", along(-k)).astype(F32)
    return mixed.astype(BF16)


def solution(mesh):
    placed = (
        P(("groups", "expert"), "blk"),
        P(("groups", "expert"), None),
        P(("groups", "expert"), None),
        P("expert", "blk", None),
        P("expert", "blk", None),
        P("expert", "blk", None),
    )
    return jax.shard_map(
        body, mesh=mesh, in_specs=placed, out_specs=P(("groups", "expert"), "blk"), check_vma=False
    )
```

```python
import functools

import jax
import jax.numpy as jnp
from jax import lax
from jax.experimental import pallas as pl
from jax.experimental.pallas import tpu as pltpu
from jax.sharding import PartitionSpec as P

FFW = 5376
PAIR = 2
LANES = 128
SLOTS = 3
MIB = 1024 * 1024
F32 = jnp.float32
BF16 = jnp.bfloat16


def largest_step(total, choices):
    for step in choices:
        if total % step == 0:
            return step
    return total


def call(kernel, outs, operands, spaces, scratch, limit, flops, moved):
    return pl.pallas_call(
        kernel,
        out_shape=outs,
        in_specs=[pl.BlockSpec(memory_space=space) for space in spaces],
        out_specs=[pl.BlockSpec(memory_space=pltpu.VMEM) for unused in outs],
        scratch_shapes=scratch,
        compiler_params=pltpu.CompilerParams(vmem_limit_bytes=limit * MIB),
        cost_estimate=pl.CostEstimate(flops=flops, bytes_accessed=moved, transcendentals=0),
    )(*operands)


def in_hbm(*arrays):
    return [pltpu.with_memory_space_constraint(array, pltpu.HBM) for array in arrays]


def columns_of(step, per, block):
    owner = lax.rem(lax.axis_index("blk") + step // per, lax.axis_size("blk"))
    return pl.ds(pl.multiple_of((owner * per + lax.rem(step, per)) * block, LANES), block)


def moves(weights, step, per, targets, sems):
    return [
        pltpu.make_async_copy(weight.at[0, :, columns_of(step, per, target.shape[-1])], target, sem)
        for weight, target, sem in zip(weights, targets, sems)
    ]


def stream(held, count, fetch, ahead, begin, from_held, from_ring):
    rest = count - held
    early, late = max(rest - SLOTS, 0), max(min(rest - SLOTS + (rest > SLOTS), rest - 1), 0)
    several = -(-len(ahead) // 2)
    for at in range(min(SLOTS, rest)):
        for copy in fetch(held + at, at):
            copy.start()
    if rest == 0:
        for copy in ahead:
            copy.start()
    begin()

    def first(step, carry):
        from_held(step)
        return carry

    if held:
        lax.fori_loop(0, held, first, 0)

    def then(at, carry):
        later = at + SLOTS - 1

        @pl.when((at > 0) & (later < rest))
        def _():
            for copy in fetch(held + later, lax.rem(later, SLOTS)):
                copy.start()

        @pl.when(at == early)
        def _():
            for copy in ahead[:several]:
                copy.start()

        @pl.when(at == late)
        def _():
            for copy in ahead[several:]:
                copy.start()

        slot = lax.rem(at, SLOTS)
        from_ring(held + at, slot, fetch(held + at, slot))
        return carry

    if rest:
        lax.fori_loop(0, rest, then, 0)


def finish(copies):
    for copy in copies:
        copy.wait()


def head_kernel(count, per, after, w_gate, w_up, gate, up, sems):
    copies = []
    for step in range(count):
        at = (sems.at[0, step], sems.at[1, step])
        copies += moves((w_gate, w_up), step, per, (gate.at[step], up.at[step]), at)
    for copy in copies:
        copy.start()
    finish(copies)


def pack_kernel(experts, tokens, ids, weights, out, held, named, weighed, sems):
    copies = [
        pltpu.make_async_copy(source, target, sems.at[at])
        for at, (source, target) in enumerate(((ids, named), (weights, weighed), (tokens, held)))
    ]
    for copy in copies:
        copy.start()
    rows, width = tokens.shape
    shape = (rows, out.shape[1] - width)
    lane = lax.broadcasted_iota(jnp.int32, shape, 1)
    diagonal = lax.broadcasted_iota(jnp.int32, (rows, rows), 0) == lax.broadcasted_iota(
        jnp.int32, (rows, rows), 1
    )
    coef = jnp.zeros(shape, F32)
    copies[0].wait()
    copies[1].wait()
    for k in range(ids.shape[0]):
        name = jnp.sum(jnp.where(diagonal, named[k : k + 1], 0), axis=1, keepdims=True)
        weight = jnp.sum(jnp.where(diagonal, weighed[k : k + 1], 0.0), axis=1, keepdims=True)
        coef += jnp.where(lax.rem(lane, experts) == name, weight, 0.0)
    high = coef.astype(BF16).astype(F32)
    middle = (coef - high).astype(BF16).astype(F32)
    low = coef - high - middle
    part = jnp.where(lane < experts, high, jnp.where(lane < 2 * experts, middle, low))
    out[:, width:] = jnp.where(lane < 3 * experts, part, 0.0).astype(BF16)
    copies[2].wait()
    out[:, :width] = held[...]


def up_kernel(kb, parts, held, more, last, *refs):
    sent, refs = refs[: 2 * len(parts)], refs[2 * len(parts) :]
    earlier, refs = (refs[:2], refs[2:]) if last else ((), refs)
    (gate_held, up_held, w_gate, w_up), refs = refs[:4], refs[4:]
    if last:
        w_down, hidden, down_next, x, gate_ring, up_ring, sems, next_sems, gate_sum, up_sum = refs
    else:
        gate_sum, up_sum, gate_next, up_next, x, gate_ring, up_ring, sems, next_sems = refs
    hid = w_gate.shape[1]
    width = x.shape[0] // len(parts)
    per = width // kb
    start = parts[0] * per
    weights = (w_gate, w_up)

    def fetch(step, slot):
        places = (gate_ring.at[slot], up_ring.at[slot])
        return moves(weights, start + step, per, places, (sems.at[0, slot], sems.at[1, slot]))

    ahead = []
    for k in range(more):
        if last:
            down_per = width // down_next.shape[-1]
            ahead += moves((w_down,), down_per + k, down_per, (down_next.at[k],), (next_sems.at[0, k],))
        else:
            places = (gate_next.at[k], up_next.at[k])
            at = (next_sems.at[0, k], next_sems.at[1, k])
            ahead += moves(weights, start + per + k, per, places, at)

    def begin():
        for j in range(len(parts)):
            rows = [sent[2 * j + at][:, :width].astype(F32) for at in range(2)]
            x[j * width : (j + 1) * width] = jnp.concatenate(rows, axis=0).T.astype(BF16)
        gate_sum[...] = earlier[0][...] if last else jnp.zeros_like(gate_sum)
        up_sum[...] = earlier[1][...] if last else jnp.zeros_like(up_sum)

    def right(step):
        return x[pl.ds(pl.multiple_of(step * kb, LANES), kb)]

    def from_held(step):
        gate_sum[...] += jnp.dot(gate_held[step], right(step), preferred_element_type=F32)
        up_sum[...] += jnp.dot(up_held[step], right(step), preferred_element_type=F32)

    def from_ring(step, slot, waits):
        waits[0].wait()
        gate_sum[...] += jnp.dot(gate_ring[slot], right(step), preferred_element_type=F32)
        waits[1].wait()
        up_sum[...] += jnp.dot(up_ring[slot], right(step), preferred_element_type=F32)

    stream(held, len(parts) * per, fetch, ahead, begin, from_held, from_ring)
    if last:
        unit = largest_step(hid, (384,))
        for first in range(0, hid, unit):
            units = pl.ds(first, unit)
            gate = gate_sum[units]
            value = gate / (1.0 + jnp.exp(-gate)) * up_sum[units]
            hidden[:, units] = value.T.astype(BF16)
    finish(ahead)


def down_kernel(width, start, count, held, more, experts, shares, hidden, own, other, *refs):
    down_held, refs = (refs[0], refs[1:]) if held else (None, refs)
    w_down, *outs, ring, sems, next_sems = refs
    down_next = outs.pop() if more else None
    unused, half, span = outs[0].shape
    fb = ring.shape[-1]
    per, inside = width // fb, span // fb
    expert = lax.axis_index("expert") // shares
    packed = jnp.concatenate([own[:, width:], other[:, width:]], axis=0).astype(F32)
    lane = lax.broadcasted_iota(jnp.int32, packed.shape, 1)
    mine = (lax.rem(lane, experts) == expert) & (lane < 3 * experts)
    coef = jnp.sum(jnp.where(mine, packed, 0.0), axis=1, keepdims=True)

    def fetch(step, slot):
        return moves((w_down,), start + step, per, (ring.at[slot],), (sems.at[slot],))

    def put(step, block):
        value = jnp.dot(hidden[...], block, preferred_element_type=F32) * coef
        columns = pl.ds(pl.multiple_of(lax.rem(step, inside) * fb, LANES), fb)
        for at, out in enumerate(outs):
            out[step // inside, :, columns] = value[at * half : (at + 1) * half].astype(out.dtype)

    def from_held(step):
        put(step, down_held[step])

    def from_ring(step, slot, waits):
        waits[0].wait()
        put(step, ring[slot])

    ahead = []
    for k in range(more):
        ahead += moves((w_down,), k, per, (down_next.at[k],), (next_sems.at[k],))
    stream(held, count, fetch, ahead, lambda: None, from_held, from_ring)
    finish(ahead)


def body(tokens, expert_ids, route_weight, w_gate, w_up, w_down):
    n_expert = lax.axis_size("expert")
    n_blk = lax.axis_size("blk")
    rows, width = tokens.shape
    top = expert_ids.shape[1]
    hid = w_gate.shape[1]
    shares = FFW // (hid * n_blk)
    experts = n_expert // shares
    places = n_expert // PAIR
    half = places * rows
    tokens_all = PAIR * half
    room = -(-3 * experts // LANES) * LANES
    vmem, hbm = pltpu.VMEM, pl.ANY
    w_gate, w_up, w_down = in_hbm(w_gate, w_up, w_down)

    (packed,) = call(
        functools.partial(pack_kernel, experts),
        [jax.ShapeDtypeStruct((rows, width + room), BF16)],
        in_hbm(tokens, expert_ids.T, route_weight.T),
        (hbm,) * 3,
        [
            pltpu.VMEM((rows, width), BF16),
            pltpu.VMEM((top, rows), jnp.int32),
            pltpu.VMEM((top, rows), F32),
            pltpu.SemaphoreType.DMA((3,)),
        ],
        8,
        rows * room,
        4 * rows * width,
    )

    def along(k):
        return [(s, ((s // PAIR + k) % places) * PAIR + s % PAIR) for s in range(n_expert)]

    def across(k):
        return [(s, (s + k) % n_blk) for s in range(n_blk)]

    def across_other(k):
        return [
            (s * n_blk + b, (s ^ 1) * n_blk + (b + k) % n_blk)
            for s in range(n_expert)
            for b in range(n_blk)
        ]

    swap = [(s, s ^ 1) for s in range(n_expert)]

    kb = largest_step(width, (512, 384, 256, 128))
    per = width // kb
    steps = per * (n_blk - 1)
    first_held, second_held, third_held = min(2, per), min(2, steps), min(3, steps)

    def blocks(count):
        return pltpu.VMEM((count, hid, kb), BF16)

    held = call(
        functools.partial(head_kernel, first_held, per),
        [blocks(first_held)] * 2,
        (packed, w_gate, w_up),
        (hbm,) * 3,
        [pltpu.SemaphoreType.DMA((2, first_held))],
        4,
        0,
        4 * hid * kb * first_held,
    )
    pieces = [packed] + [lax.ppermute(packed, "expert", along(k)) for k in range(1, places)]
    pieces, held = lax.optimization_barrier((pieces, held))
    own = jnp.concatenate(pieces, axis=0)
    other = lax.ppermute(own, "expert", swap)
    bare = own[:, :width]
    sent = []
    for j in range(1, n_blk):
        sent.append(lax.ppermute(bare, "blk", across(-j)))
        sent.append(lax.ppermute(bare, ("expert", "blk"), across_other(-j)))

    sums = [jax.ShapeDtypeStruct((hid, tokens_all), F32)] * 2

    def up(parts, held, more, last, outs, operands):
        weights = (w_gate, w_up, w_down) if last else (w_gate, w_up)
        return call(
            functools.partial(up_kernel, kb, parts, held, more, last),
            outs,
            (*operands, *weights),
            (vmem,) * len(operands) + (hbm,) * len(weights),
            [
                pltpu.VMEM((width * len(parts), tokens_all), BF16),
                blocks(SLOTS),
                blocks(SLOTS),
                pltpu.SemaphoreType.DMA((2, SLOTS)),
                pltpu.SemaphoreType.DMA((2, more)),
            ]
            + [pltpu.VMEM(each.shape, F32) for each in sums if last],
            23 if last else 20,
            4 * tokens_all * hid * width * len(parts),
            4 * hid * width * len(parts),
        )

    *partial_sums, gate_held, up_held = up(
        (0,), first_held, second_held, False, sums + [blocks(second_held)] * 2, (own, other, *held)
    )
    hidden, down_held = up(
        tuple(range(1, n_blk)),
        second_held,
        third_held,
        True,
        [jax.ShapeDtypeStruct((tokens_all, hid), BF16), blocks(third_held)],
        (*sent, *partial_sums, gate_held, up_held),
    )

    def down(hidden, first, count, more, *down_held):
        held = down_held[0].shape[0] if down_held else 0
        span = min(count, per)
        shape = (count // span, half, span * kb)
        return call(
            functools.partial(down_kernel, width, first, count, held, more, experts, shares),
            [jax.ShapeDtypeStruct(shape, F32), jax.ShapeDtypeStruct(shape, BF16)] + [blocks(more)] * (more > 0),
            (hidden, own, other, *down_held, w_down),
            (vmem,) * (3 + len(down_held)) + (hbm,),
            [
                blocks(min(SLOTS, max(count - held, 1))),
                pltpu.SemaphoreType.DMA((SLOTS,)),
                pltpu.SemaphoreType.DMA((max(more, 1),)),
            ],
            14,
            2 * tokens_all * hid * kb * count,
            2 * hid * kb * count,
        )

    early = per // 3
    away, given, *early_held = down(hidden, per, steps, early, down_held)
    given = lax.ppermute(given, "expert", swap)
    parts = [down(hidden, 0, early, 0, *early_held)] if early else []
    away = (away + given.astype(F32)).astype(BF16)
    away, hidden = lax.optimization_barrier((away, hidden))
    away = jnp.pad(away, ((0, 0), (0, 0), (0, room)))
    total = [lax.ppermute(away[j - 1], "blk", across(j))[:, :width] for j in range(1, n_blk)]
    parts.append(down(hidden, early, per - early, 0))
    kept, given = (jnp.concatenate([part[at][0] for part in parts], axis=1) for at in range(2))
    summed = kept + lax.ppermute(given, "expert", swap).astype(F32)
    for term in total:
        summed = summed + term.astype(F32)
    mixed = summed[:rows]
    for k in range(1, places):
        piece = summed[k * rows : (k + 1) * rows].astype(BF16)
        mixed = mixed + lax.ppermute(piece, "expert", along(-k)).astype(F32)
    return mixed.astype(BF16)


def solution(mesh):
    placed = (
        P(("groups", "expert"), "blk"),
        P(("groups", "expert"), None),
        P(("groups", "expert"), None),
        P("expert", "blk", None),
        P("expert", "blk", None),
        P("expert", "blk", None),
    )
    return jax.shard_map(
        body, mesh=mesh, in_specs=placed, out_specs=P(("groups", "expert"), "blk"), check_vma=False
    )
```
